32 devices in a mesh: orb: 32 (over z, y, x, core).
Axes of the slice: x: 2, y: 2, z: 4, core: 2. Of those that a mesh axis runs over, the one named last changes fastest.
Arguments:
- orbitals: bfloat16 [32, 48, 2304], P('orb'), may hold values from -6 to 6
- pair_mask: int32 [2, 32], replicated, may hold values from 0 to 1, as said below
- offsets: int32 [3, 2, 32], replicated, may hold values from -12 to 12
Outputs:
- exchange: bfloat16 [32, 48, 2304], P('orb')
The draws below stay inside these ranges and needn't reach their ends.
Inputs may be any that keep to these rules, and one draw needn't show every extreme that they name: `pair_mask`: in every matching, the pair that holds orbital 0 and the pair that holds orbital 32 - 1 are live.
All inputs are finite; a program needn't handle non-finite values.
Results may differ from the reference program's by a relative error of at most 0.004.
Values may be sent and summed in bfloat16 or wider, within the bound.
A program may use at most 64 MiB of HBM per device.

```python
import math
import jax
import jax.numpy as jnp
import numpy as np
from jax import lax

BOX = 48
MATCH = 2
ORBITALS = 32
OMAX = 12
N_ORB = 32


def draw_pair_mask(key, part):
    mixed = jax.random.fold_in(key, 7301)
    values = jax.random.randint(mixed, (MATCH, ORBITALS), 0, 4, dtype=jnp.int32)
    live = jnp.where(values < 3, 1, 0).astype(jnp.int32)
    levels = ORBITALS.bit_length() - 1
    places = jnp.arange(ORBITALS, dtype=jnp.int32)
    rows = []
    for match_index in range(MATCH):
        bit_pos = match_index * (levels - 1) // (MATCH - 1)
        top_lower = ORBITALS - 1 - (1 << bit_pos)
        forced = (places == 0) | (places == top_lower)
        rows.append(jnp.where(forced, 1, live[match_index]).astype(jnp.int32))
    return jnp.stack(rows, axis=0)


def touch_ends(result, stream_key, low, high):
    shape = result.shape
    index_at = [jax.random.randint(jax.random.fold_in(stream_key, axis), (), 0, shape[axis]) for axis in range(len(shape))]
    result = result.at[tuple(index_at)].set(low)
    longest = shape.index(max(shape))
    index_at[longest] = (index_at[longest] + 1) % shape[longest]
    return result.at[tuple(index_at)].set(high)


def block_scale(rng, shape, cuts, low, high):
    level = 1.0
    for axis_at, shards_of in cuts:
        heights = jax.random.uniform(jax.random.fold_in(jax.random.fold_in(rng, 6), axis_at), (shards_of,), jnp.float32, low / len(cuts), high / len(cuts))
        level = level * jnp.repeat(jnp.exp(heights), shape[axis_at] // shards_of).reshape((-1,) + (1,) * (len(shape) - 1 - axis_at))
    return level


def scatter_about(own_key, shape, deviation, most, split=(), kind=jnp.bfloat16):
    level = block_scale(own_key, shape, split, -0.22, 0.18) if split else 1.0
    values = jax.random.normal(own_key, shape, jnp.float32) * deviation * level
    return jnp.minimum(jnp.maximum(values, -most), most).astype(kind)


def setup_inputs(seed: int = 0) -> dict:
    arg_keys = jax.random.split(jax.random.key(seed), 4)
    return {
        "orbitals": scatter_about(arg_keys[0], (ORBITALS, BOX, BOX * BOX), 1.0, 6.0, ((0, 32),)),
        "pair_mask": draw_pair_mask(jax.random.fold_in(arg_keys[3], 71), 0),
        "offsets": touch_ends(jax.random.randint(arg_keys[2], (3, MATCH, ORBITALS), -OMAX, OMAX + 1), jax.random.fold_in(arg_keys[2], 1), -OMAX, OMAX).astype(jnp.int32),
    }


screening = 0.5

def sine_table(extent):
    modes = jnp.arange(1, extent + 1, dtype=jnp.int32).astype(jnp.float32)
    angles = math.pi * modes[:, None] * modes[None, :] / (extent + 1)
    return math.sqrt(2.0 / (extent + 1)) * jnp.sin(angles)

def inverse_symbol(extent):
    modes = jnp.arange(1, extent + 1, dtype=jnp.int32).astype(jnp.float32)
    eigenvalue = 2.0 - 2.0 * jnp.cos(math.pi * modes / (extent + 1))
    summed_eigen = eigenvalue[:, None, None] + eigenvalue[None, :, None] + eigenvalue[None, None, :]
    return 1.0 / (summed_eigen + screening)

def transform(volume, sines):
    exact = lax.Precision.HIGHEST
    volume = jnp.einsum('ai,ijk->ajk', sines, volume, precision=exact)
    volume = jnp.einsum('bj,ajk->abk', sines, volume, precision=exact)
    return jnp.einsum('ck,abk->abc', sines, volume, precision=exact)

def shift_box(volume, offset):
    extent = volume.shape[0]
    places = jnp.arange(extent, dtype=jnp.int32)
    for axis_pos in range(3):
        volume = jnp.roll(volume, offset[axis_pos], axis=axis_pos)
        source = places - offset[axis_pos]
        inside = (source >= 0) & (source < extent)
        view_shape = [1, 1, 1]
        view_shape[axis_pos] = extent
        volume = jnp.where(inside.reshape(view_shape), volume, jnp.zeros_like(volume))
    return volume

def pair_terms(phi_low, phi_up, offset, sines, symbol):
    visitor = shift_box(phi_up, offset)
    density = phi_low * visitor
    potential = transform(symbol * transform(density, sines), sines)
    lower_term = (potential * visitor).astype(jnp.bfloat16)
    upper_term = shift_box(potential * phi_low, -offset).astype(jnp.bfloat16)
    return (lower_term, upper_term)

def reference(orbitals, pair_mask, offsets):
    volumes = orbitals.reshape(ORBITALS, BOX, BOX, BOX)
    sines = sine_table(BOX)
    symbol = inverse_symbol(BOX)
    levels = N_ORB.bit_length() - 1
    everyone = np.arange(ORBITALS)
    summed = jnp.zeros((ORBITALS, BOX, BOX, BOX), jnp.float32)
    for match_index in range(MATCH):
        bit_pos = match_index * (levels - 1) // (MATCH - 1)
        lowers = everyone[(everyone >> bit_pos) % 2 == 0]
        uppers = lowers + (1 << bit_pos)

        def one_pair(items):
            low_orb, up_orb, offset, live = items
            lower_term, upper_term = pair_terms(low_orb.astype(jnp.float32), up_orb.astype(jnp.float32), offset, sines, symbol)
            lower_term = jnp.where(live > 0, lower_term, jnp.zeros_like(lower_term))
            upper_term = jnp.where(live > 0, upper_term, jnp.zeros_like(upper_term))
            return (lower_term, upper_term)
        pair_offsets = jnp.transpose(offsets[:, match_index, lowers]).astype(jnp.int32)
        lower_all, upper_all = lax.map(one_pair, (volumes[lowers], volumes[uppers], pair_offsets, pair_mask[match_index, lowers]))
        summed = summed.at[lowers].add(lower_all.astype(jnp.float32))
        summed = summed.at[uppers].add(upper_all.astype(jnp.float32))
    return (-summed).astype(jnp.bfloat16).reshape(ORBITALS, BOX, BOX * BOX)
```

```python
import functools
import math

import jax
import jax.numpy as jnp
import ml_dtypes
import numpy as np
from jax import lax
from jax.experimental import pallas as pl
from jax.experimental.pallas import tpu as pltpu
from jax.sharding import PartitionSpec as P

screening = 0.5
MESH = pl.DeviceIdType.MESH
NT = (((1,), (1,)), ((), ()))
LANES = 128


def split(values):
    high = values.astype(jnp.bfloat16)
    low = (values - high.astype(jnp.float32)).astype(jnp.bfloat16)
    return high, low


def split_constant(values):
    high = values.astype(ml_dtypes.bfloat16)
    low = (values - high.astype(np.float64)).astype(ml_dtypes.bfloat16)
    return high, low


def tables(extent):
    modes = np.arange(1, extent + 1, dtype=np.float64)
    sines = math.sqrt(2.0 / (extent + 1)) * np.sin(
        math.pi * modes[:, None] * modes[None, :] / (extent + 1)
    )
    eigenvalue = 2.0 - 2.0 * np.cos(math.pi * modes / (extent + 1))
    high, low = split_constant(sines)
    stacked = np.zeros((2 * extent, LANES), ml_dtypes.bfloat16)
    stacked[:extent, :extent] = high
    stacked[extent:, :extent] = low
    width = math.lcm(extent, LANES)
    blocks = np.kron(np.eye(width // extent), sines)
    blocks_high, blocks_low = split_constant(blocks)
    lane = np.arange(extent * extent)
    middle, minor = lane // extent, lane % extent
    eigen_lane = (eigenvalue[middle] + eigenvalue[minor] + screening)[None].astype(np.float32)
    eigen_row = np.broadcast_to(eigenvalue[:, None], (extent, LANES)).astype(np.float32)
    places = np.stack([middle, minor]).astype(np.int32)
    return stacked, blocks_high, blocks_low, eigen_row, eigen_lane, places


def kernel(
    strides,
    pieces,
    offsets_ref,
    mask_ref,
    orbital_ref,
    sines_ref,
    blocks_high_ref,
    blocks_low_ref,
    eigen_row_ref,
    eigen_lane_ref,
    places_ref,
    out_ref,
    own,
    arrived,
    dense,
    slabs,
    symbol,
    load_sem,
    send_sem,
    recv_sem,
):
    extent, cells = own.shape
    width = blocks_high_ref.shape[0]
    myself = lax.axis_index("orb")
    lows = [lax.rem(myself // stride, 2) == 0 for stride in strides]
    partners = [
        jnp.where(low, myself + stride, myself - stride) for low, stride in zip(lows, strides)
    ]

    load = pltpu.make_async_copy(orbital_ref, own, load_sem)
    load.start()
    barrier = pltpu.get_barrier_semaphore()
    for partner in partners:
        pl.semaphore_signal(barrier, inc=1, device_id={"orb": partner}, device_id_type=MESH)
    pl.semaphore_wait(barrier, len(strides))
    rows = extent // pieces
    copies = [[] for _ in strides]
    for match_index in sorted(range(len(strides)), key=lambda at: -strides[at]):
        for piece in range(pieces):
            span = pl.ds(piece * rows, rows)
            copy = pltpu.make_async_remote_copy(
                src_ref=orbital_ref.at[span],
                dst_ref=arrived.at[match_index, span],
                send_sem=send_sem.at[match_index, piece],
                recv_sem=recv_sem.at[match_index, piece],
                device_id={"orb": partners[match_index]},
                device_id_type=MESH,
            )
            copy.start()
            copies[match_index].append(copy)
    load.wait()

    symbol[...] = 1.0 / (eigen_row_ref[:, :1] + eigen_lane_ref[...])
    dense[:, cells:] = jnp.zeros((extent, LANES), jnp.float32)

    def contract_rows(volume):
        high, low = split(volume)
        both = jnp.dot(
            sines_ref[:, :extent], high, preferred_element_type=jnp.float32
        )
        rest = jnp.dot(sines_ref[:extent, :extent], low, preferred_element_type=jnp.float32)
        return both[:extent] + (both[extent:] + rest)

    def contract_lanes(volume):
        chunks = cells // width
        tall = jnp.concatenate(
            [volume[:, at * width : (at + 1) * width] for at in range(chunks)], axis=0
        )
        high, low = split(tall)
        result = jnp.dot(high, blocks_high_ref[...], preferred_element_type=jnp.float32)
        result += jnp.dot(high, blocks_low_ref[...], preferred_element_type=jnp.float32)
        result += jnp.dot(low, blocks_high_ref[...], preferred_element_type=jnp.float32)
        return jnp.concatenate(
            [result[at * extent : (at + 1) * extent] for at in range(chunks)], axis=1
        )

    def rotate(volume):
        dense[:, :cells] = volume
        for at in range(extent):
            slabs[pl.ds(at, extent, stride=extent), :] = dense[:, at * extent : at * extent + LANES]
        high, low = split(slabs[...])
        both = lax.dot_general(sines_ref[...], high, NT, preferred_element_type=jnp.float32)
        rest = lax.dot_general(
            sines_ref[:extent, :], low, NT, preferred_element_type=jnp.float32
        )
        return both[:extent] + (both[extent:] + rest)

    def solve(density):
        spectrum = contract_lanes(rotate(contract_rows(density)))
        return contract_lanes(rotate(rotate(symbol[...] * spectrum)))

    def shift_box(volume, offset):
        row = lax.broadcasted_iota(jnp.int32, (extent, extent), 0)
        column = lax.broadcasted_iota(jnp.int32, (extent, extent), 1)
        pick = jnp.where(row - column == offset[0], 1.0, 0.0).astype(jnp.bfloat16)
        moved = jnp.dot(pick, volume.astype(jnp.bfloat16), preferred_element_type=jnp.float32)
        turn = offset[1] * extent + offset[2]
        moved = pltpu.roll(moved, jnp.where(turn < 0, turn + cells, turn), 1)
        middle = places_ref[0:1, :] - offset[1]
        minor = places_ref[1:2, :] - offset[2]
        inside = (middle >= 0) & (middle < extent) & (minor >= 0) & (minor < extent)
        return jnp.where(inside, moved, 0.0)

    total = None
    for match_index, stride in enumerate(strides):
        is_low = lows[match_index]
        lower = jnp.where(is_low, myself, myself - stride)
        live = mask_ref[match_index, lower]
        offset = [offsets_ref[axis, match_index, lower] for axis in range(3)]
        for copy in copies[match_index]:
            copy.wait_recv()
        mine = own[...].astype(jnp.float32)
        theirs = arrived[match_index].astype(jnp.float32)
        phi_low = jnp.where(is_low, mine, theirs)
        visitor = shift_box(jnp.where(is_low, theirs, mine), offset)
        potential = solve(phi_low * visitor)
        term = (potential * jnp.where(is_low, visitor, phi_low)).astype(jnp.bfloat16)
        term = term.astype(jnp.float32)
        back = [jnp.where(is_low, 0, -value) for value in offset]
        term = jnp.where(live > 0, shift_box(term, back), 0.0)
        total = term if total is None else total + term
    out_ref[...] = (-total).astype(out_ref.dtype)
    for started in copies:
        for copy in started:
            copy.wait_send()


def per_device(orbitals, pair_mask, offsets):
    extent, cells = orbitals.shape[1:]
    levels = lax.axis_size("orb").bit_length() - 1
    matches = pair_mask.shape[0]
    strides = [1 << match_index * (levels - 1) // (matches - 1) for match_index in range(matches)]
    pieces = extent // 16
    vmem = pl.BlockSpec(memory_space=pltpu.VMEM)
    smem = pl.BlockSpec(memory_space=pltpu.SMEM)
    exchange = pl.pallas_call(
        functools.partial(kernel, strides, pieces),
        out_shape=jax.ShapeDtypeStruct((extent, cells), jnp.bfloat16),
        in_specs=[smem, smem, pl.BlockSpec(memory_space=pl.ANY)] + [vmem] * 6,
        out_specs=vmem,
        scratch_shapes=[
            pltpu.VMEM((extent, cells), jnp.bfloat16),
            pltpu.VMEM((matches, extent, cells), jnp.bfloat16),
            pltpu.VMEM((extent, cells + LANES), jnp.float32),
            pltpu.VMEM((cells, LANES), jnp.float32),
            pltpu.VMEM((extent, cells), jnp.float32),
            pltpu.SemaphoreType.DMA,
            pltpu.SemaphoreType.DMA((matches, pieces)),
            pltpu.SemaphoreType.DMA((matches, pieces)),
        ],
        compiler_params=pltpu.CompilerParams(
            collective_id=0, has_side_effects=True, vmem_limit_bytes=40 * 1024 * 1024
        ),
        name="exchange",
    )(offsets, pair_mask, orbitals.reshape(extent, cells), *map(jnp.asarray, tables(extent)))
    return exchange.reshape(1, extent, cells)


def solution(mesh):
    placed = (P("orb", None, None), P(), P())
    return jax.shard_map(
        per_device, mesh=mesh, in_specs=placed, out_specs=P("orb", None, None), check_vma=False
    )
```

```python
import functools
import math

import jax
import jax.numpy as jnp
import ml_dtypes
import numpy as np
from jax import lax
from jax.experimental import pallas as pl
from jax.experimental.pallas import tpu as pltpu
from jax.sharding import PartitionSpec as P

screening = 0.5
MESH = pl.DeviceIdType.MESH
NT = (((1,), (1,)), ((), ()))
LANES = 128


def split(values):
    high = values.astype(jnp.bfloat16)
    low = (values - high.astype(jnp.float32)).astype(jnp.bfloat16)
    return high, low


def split_constant(values):
    high = values.astype(ml_dtypes.bfloat16)
    low = (values - high.astype(np.float64)).astype(ml_dtypes.bfloat16)
    return high, low


def tables(extent):
    modes = np.arange(1, extent + 1, dtype=np.float64)
    sines = math.sqrt(2.0 / (extent + 1)) * np.sin(
        math.pi * modes[:, None] * modes[None, :] / (extent + 1)
    )
    eigenvalue = 2.0 - 2.0 * np.cos(math.pi * modes / (extent + 1))
    high, low = split_constant(sines)
    stacked = np.zeros((2 * extent, LANES), ml_dtypes.bfloat16)
    stacked[:extent, :extent] = high
    stacked[extent:, :extent] = low
    width = math.lcm(extent, LANES)
    blocks = np.kron(np.eye(width // extent), sines)
    blocks_high, blocks_low = split_constant(blocks)
    lane = np.arange(extent * extent)
    middle, minor = lane // extent, lane % extent
    eigen_lane = (eigenvalue[middle] + eigenvalue[minor] + screening)[None].astype(np.float32)
    eigen_row = np.broadcast_to(eigenvalue[:, None], (extent, LANES)).astype(np.float32)
    places = np.stack([middle, minor]).astype(np.int32)
    return stacked, blocks_high, blocks_low, eigen_row, eigen_lane, places


def kernel(
    strides,
    pieces,
    orbital_ref,
    *refs,
):
    count = (len(refs) - 9) // 2
    sources, out_ref, held = refs[:count], refs[count], refs[count + 1 : 2 * count + 1]
    own, arrived, dense, slabs, symbol, load_sem, send_sem, recv_sem = refs[2 * count + 1 :]
    offsets_ref, mask_ref, sines_ref, blocks_high_ref, blocks_low_ref = held[:5]
    eigen_row_ref, eigen_lane_ref, places_ref = held[5:]
    extent, cells = own.shape
    width = blocks_high_ref.shape[0]
    myself = lax.axis_index("orb")
    lows = [lax.rem(myself // stride, 2) == 0 for stride in strides]
    partners = [
        jnp.where(low, myself + stride, myself - stride) for low, stride in zip(lows, strides)
    ]

    loads = [
        pltpu.make_async_copy(source, target, load_sem.at[at])
        for at, (source, target) in enumerate(zip((orbital_ref, *sources), (own, *held)))
    ]
    barrier = pltpu.get_barrier_semaphore()
    for partner in partners:
        pl.semaphore_signal(barrier, inc=1, device_id={"orb": partner}, device_id_type=MESH)
    for load in loads:
        load.start()
    pl.semaphore_wait(barrier, len(strides))
    rows = extent // pieces
    copies = [[] for _ in strides]
    for match_index in sorted(range(len(strides)), key=lambda at: -strides[at]):
        for piece in range(pieces):
            span = pl.ds(piece * rows, rows)
            copy = pltpu.make_async_remote_copy(
                src_ref=orbital_ref.at[span],
                dst_ref=arrived.at[match_index, span],
                send_sem=send_sem.at[match_index, piece],
                recv_sem=recv_sem.at[match_index, piece],
                device_id={"orb": partners[match_index]},
                device_id_type=MESH,
            )
            copy.start()
            copies[match_index].append(copy)
    for load in loads:
        load.wait()

    symbol[...] = 1.0 / (eigen_row_ref[:, :1] + eigen_lane_ref[...])
    dense[:, cells:] = jnp.zeros((extent, LANES), jnp.float32)

    def contract_rows(volume):
        high, low = split(volume)
        both = jnp.dot(
            sines_ref[:, :extent], high, preferred_element_type=jnp.float32
        )
        rest = jnp.dot(sines_ref[:extent, :extent], low, preferred_element_type=jnp.float32)
        return both[:extent] + (both[extent:] + rest)

    def contract_lanes(volume):
        chunks = cells // width
        tall = jnp.concatenate(
            [volume[:, at * width : (at + 1) * width] for at in range(chunks)], axis=0
        )
        high, low = split(tall)
        result = jnp.dot(high, blocks_high_ref[...], preferred_element_type=jnp.float32)
        result += jnp.dot(high, blocks_low_ref[...], preferred_element_type=jnp.float32)
        result += jnp.dot(low, blocks_high_ref[...], preferred_element_type=jnp.float32)
        return jnp.concatenate(
            [result[at * extent : (at + 1) * extent] for at in range(chunks)], axis=1
        )

    def rotate(volume):
        dense[:, :cells] = volume
        for at in range(extent):
            slabs[pl.ds(at, extent, stride=extent), :] = dense[:, at * extent : at * extent + LANES]
        high, low = split(slabs[...])
        both = lax.dot_general(sines_ref[...], high, NT, preferred_element_type=jnp.float32)
        rest = lax.dot_general(
            sines_ref[:extent, :], low, NT, preferred_element_type=jnp.float32
        )
        return both[:extent] + (both[extent:] + rest)

    def solve(density):
        spectrum = contract_lanes(rotate(contract_rows(density)))
        return contract_lanes(rotate(rotate(symbol[...] * spectrum)))

    def shift_box(volume, offset):
        row = lax.broadcasted_iota(jnp.int32, (extent, extent), 0)
        column = lax.broadcasted_iota(jnp.int32, (extent, extent), 1)
        pick = jnp.where(row - column == offset[0], 1.0, 0.0).astype(jnp.bfloat16)
        moved = jnp.dot(pick, volume.astype(jnp.bfloat16), preferred_element_type=jnp.float32)
        turn = offset[1] * extent + offset[2]
        moved = pltpu.roll(moved, jnp.where(turn < 0, turn + cells, turn), 1)
        middle = places_ref[0:1, :] - offset[1]
        minor = places_ref[1:2, :] - offset[2]
        inside = (middle >= 0) & (middle < extent) & (minor >= 0) & (minor < extent)
        return jnp.where(inside, moved, 0.0)

    total = None
    for match_index, stride in enumerate(strides):
        is_low = lows[match_index]
        lower = jnp.where(is_low, myself, myself - stride)
        live = mask_ref[match_index, lower]
        offset = [offsets_ref[axis, match_index, lower] for axis in range(3)]
        for copy in copies[match_index]:
            copy.wait_recv()
        mine = own[...].astype(jnp.float32)
        theirs = arrived[match_index].astype(jnp.float32)
        phi_low = jnp.where(is_low, mine, theirs)
        visitor = shift_box(jnp.where(is_low, theirs, mine), offset)
        potential = solve(phi_low * visitor)
        term = (potential * jnp.where(is_low, visitor, phi_low)).astype(jnp.bfloat16)
        term = term.astype(jnp.float32)
        back = [jnp.where(is_low, 0, -value) for value in offset]
        term = jnp.where(live > 0, shift_box(term, back), 0.0)
        total = term if total is None else total + term
    out_ref[...] = (-total).astype(out_ref.dtype)
    for started in copies:
        for copy in started:
            copy.wait_send()


def per_device(orbitals, pair_mask, offsets):
    extent, cells = orbitals.shape[1:]
    levels = lax.axis_size("orb").bit_length() - 1
    matches = pair_mask.shape[0]
    strides = [1 << match_index * (levels - 1) // (matches - 1) for match_index in range(matches)]
    pieces = extent // 16
    operands = (offsets, pair_mask, *map(jnp.asarray, tables(extent)))
    spaces = [pltpu.SMEM] * 2 + [pltpu.VMEM] * (len(operands) - 2)
    exchange = pl.pallas_call(
        functools.partial(kernel, strides, pieces),
        out_shape=jax.ShapeDtypeStruct((extent, cells), jnp.bfloat16),
        in_specs=[pl.BlockSpec(memory_space=pltpu.HBM)] * (1 + len(operands)),
        out_specs=pl.BlockSpec(memory_space=pltpu.VMEM),
        scratch_shapes=[space(one.shape, one.dtype) for space, one in zip(spaces, operands)]
        + [
            pltpu.VMEM((extent, cells), jnp.bfloat16),
            pltpu.VMEM((matches, extent, cells), jnp.bfloat16),
            pltpu.VMEM((extent, cells + LANES), jnp.float32),
            pltpu.VMEM((cells, LANES), jnp.float32),
            pltpu.VMEM((extent, cells), jnp.float32),
            pltpu.SemaphoreType.DMA((1 + len(operands),)),
            pltpu.SemaphoreType.DMA((matches, pieces)),
            pltpu.SemaphoreType.DMA((matches, pieces)),
        ],
        compiler_params=pltpu.CompilerParams(
            collective_id=0, has_side_effects=True, vmem_limit_bytes=64 * 1024 * 1024
        ),
        name="exchange",
    )(orbitals.reshape(extent, cells), *operands)
    return exchange.reshape(1, extent, cells)


def solution(mesh):
    placed = (P("orb", None, None), P(), P())
    return jax.shard_map(
        per_device, mesh=mesh, in_specs=placed, out_specs=P("orb", None, None), check_vma=False
    )
```

```python
import functools
import math

import jax
import jax.numpy as jnp
import ml_dtypes
import numpy as np
from jax import lax
from jax.experimental import pallas as pl
from jax.experimental.pallas import tpu as pltpu
from jax.sharding import PartitionSpec as P

screening = 0.5
MESH = pl.DeviceIdType.MESH
LANES = 128


def split(values):
    high = values.astype(jnp.bfloat16)
    low = (values - high.astype(jnp.float32)).astype(jnp.bfloat16)
    return high, low


def split_constant(values):
    high = values.astype(ml_dtypes.bfloat16)
    low = (values - high.astype(np.float64)).astype(ml_dtypes.bfloat16)
    return high, low


def tables(extent):
    modes = np.arange(1, extent + 1, dtype=np.float64)
    sines = math.sqrt(2.0 / (extent + 1)) * np.sin(
        math.pi * modes[:, None] * modes[None, :] / (extent + 1)
    )
    eigenvalue = 2.0 - 2.0 * np.cos(math.pi * modes / (extent + 1))
    width = math.lcm(extent, LANES)
    blocks = np.kron(np.eye(width // extent), sines)
    last = np.zeros(LANES)
    last[:extent] = eigenvalue
    eigen_lane = (eigenvalue[:, None] + last[None, :] + screening).reshape(1, extent * LANES)
    eigen_row = np.broadcast_to(eigenvalue[:, None], (extent, LANES))
    lane = np.arange(extent * extent)
    places = np.stack([lane // extent, lane % extent]).astype(np.int32)
    return (
        *split_constant(sines),
        *split_constant(blocks),
        eigen_row.astype(np.float32),
        eigen_lane.astype(np.float32),
        places,
    )


def kernel(
    strides,
    pieces,
    orbital_ref,
    *refs,
):
    count = (len(refs) - 11) // 2
    sources, out_ref, held = refs[:count], refs[count], refs[count + 1 : 2 * count + 1]
    own, arrived, rows_in, rows_out, flat, symbol, moved_own, load_sem, send_sem, recv_sem = refs[
        2 * count + 1 :
    ]
    offsets_ref, mask_ref, sines_high_ref, sines_low_ref, blocks_high_ref, blocks_low_ref = held[:6]
    eigen_row_ref, eigen_lane_ref, places_ref = held[6:]
    extent, cells = own.shape
    width = blocks_high_ref.shape[0]
    myself = lax.axis_index("orb")
    lows = [lax.rem(myself // stride, 2) == 0 for stride in strides]
    partners = [
        jnp.where(low, myself + stride, myself - stride) for low, stride in zip(lows, strides)
    ]

    loads = [
        pltpu.make_async_copy(source, target, load_sem.at[at])
        for at, (source, target) in enumerate(zip((orbital_ref, *sources), (own, *held)))
    ]
    barrier = pltpu.get_barrier_semaphore()
    for partner in partners:
        pl.semaphore_signal(barrier, inc=1, device_id={"orb": partner}, device_id_type=MESH)
    for load in loads:
        load.start()
    pl.semaphore_wait(barrier, len(strides))
    copies = [[] for _ in strides]
    for match_index in sorted(range(len(strides)), key=lambda at: -strides[at]):
        for piece in range(pieces):
            span = pl.ds(piece * width, width)
            copy = pltpu.make_async_remote_copy(
                src_ref=orbital_ref.at[:, span],
                dst_ref=arrived.at[match_index, :, span],
                send_sem=send_sem.at[match_index, piece],
                recv_sem=recv_sem.at[match_index, piece],
                device_id={"orb": partners[match_index]},
                device_id_type=MESH,
            )
            copy.start()
            copies[match_index].append(copy)
    for load in loads:
        load.wait()

    symbol[...] = 1.0 / (eigen_row_ref[:, :1] + eigen_lane_ref[...])
    per_width = width // extent

    def product(left, right):
        return jnp.dot(left, right, preferred_element_type=jnp.float32)

    def side_by_side(high, low):
        return jnp.concatenate([high, low, high], axis=1).astype(jnp.bfloat16)

    row = lax.broadcasted_iota(jnp.int32, (extent, extent), 0)
    column = lax.broadcasted_iota(jnp.int32, (extent, extent), 1)
    wide_row = lax.broadcasted_iota(jnp.int32, (width, width), 0)
    wide_column = lax.broadcasted_iota(jnp.int32, (width, width), 1)
    wide_minor = places_ref[1:2, :width]

    def forward_table(amount):
        pick = jnp.where(row - column == amount, 1.0, 0.0).astype(jnp.bfloat16)
        return side_by_side(product(sines_high_ref[...], pick), product(sines_low_ref[...], pick))

    def inverse_table(amount):
        pick = jnp.where(column - row == amount, 1.0, 0.0).astype(jnp.bfloat16)
        return side_by_side(product(pick, sines_high_ref[...]), product(pick, sines_low_ref[...]))

    def forward_blocks(amount):
        same = (wide_minor >= amount) & (wide_minor < extent + amount)
        pick = jnp.where((wide_column - wide_row == amount) & same, 1.0, 0.0).astype(jnp.bfloat16)
        high, low = product(pick, blocks_high_ref[...]), product(pick, blocks_low_ref[...])
        return high.astype(jnp.bfloat16), low.astype(jnp.bfloat16)

    def inverse_blocks(amount):
        same = (wide_minor >= -amount) & (wide_minor < extent - amount)
        pick = jnp.where((wide_row - wide_column == amount) & same, 1.0, 0.0).astype(jnp.bfloat16)
        high, low = product(blocks_high_ref[...], pick), product(blocks_low_ref[...], pick)
        return high.astype(jnp.bfloat16), low.astype(jnp.bfloat16)

    def contract_rows(table, volume):
        high, low = split(volume)
        return product(table, jnp.concatenate([high, high, low], axis=0))

    def contract_lanes(blocks, volume):
        chunks = volume.shape[1] // width
        tall = [volume[:, at * width : (at + 1) * width] for at in range(chunks)]
        high, low = split(jnp.concatenate(tall, axis=0))
        result = product(high, blocks[0]) + (product(high, blocks[1]) + product(low, blocks[0]))
        parts = [result[at * extent : (at + 1) * extent] for at in range(chunks)]
        return jnp.concatenate(parts, axis=1)

    def shift_box(volume, offset):
        pick = jnp.where(row - column == offset[0], 1.0, 0.0).astype(jnp.bfloat16)
        moved = product(pick, volume)
        turn = offset[1] * extent + offset[2]
        moved = pltpu.roll(moved, jnp.where(turn < 0, turn + cells, turn), 1)
        middle = places_ref[0:1, :] - offset[1]
        minor = places_ref[1:2, :] - offset[2]
        inside = (middle >= 0) & (middle < extent) & (minor >= 0) & (minor < extent)
        return jnp.where(inside, moved, 0.0)

    total = None
    for match_index, stride in enumerate(strides):
        is_low = lows[match_index]
        lower = jnp.where(is_low, myself, myself - stride)
        live = mask_ref[match_index, lower]
        offset = [offsets_ref[axis, match_index, lower] for axis in range(3)]
        ahead = [jnp.where(is_low, value, 0) for value in offset]
        behind = [jnp.where(is_low, 0, value) for value in offset]
        outward = [jnp.where(is_low, -value, value) for value in offset]
        moved_own[...] = shift_box(own[...], outward)
        rows_forward, middle_forward = forward_table(ahead[0]), forward_table(ahead[1])
        rows_inverse, middle_inverse = inverse_table(behind[0]), inverse_table(behind[1])
        lanes_forward, lanes_inverse = forward_blocks(ahead[2]), inverse_blocks(behind[2])

        for piece, copy in enumerate(copies[match_index]):
            copy.wait_recv()
            span = slice(piece * width, (piece + 1) * width)
            density = arrived[match_index, :, span].astype(jnp.float32) * moved_own[:, span]
            part = contract_lanes(lanes_forward, contract_rows(rows_forward, density))
            part = jnp.concatenate([part, part[:, :LANES]], axis=1)
            for at in range(per_width):
                rows_in[pl.ds(piece * per_width + at, extent, stride=extent), :] = part[
                    :, at * extent : at * extent + LANES
                ]
        volume = jnp.concatenate(
            [rows_in[at * extent : (at + 1) * extent, :] for at in range(extent)], axis=1
        )
        volume = symbol[...] * contract_rows(middle_forward, volume)
        volume = contract_rows(middle_inverse, volume)
        for at in range(extent):
            rows_out[at * extent : (at + 1) * extent, :] = volume[:, at * LANES : (at + 1) * LANES]
        for at in range(extent):
            flat[:, at * extent : (at + 1) * extent] = rows_out[
                pl.ds(at, extent, stride=extent), :
            ][:, :extent]
        potential = contract_lanes(lanes_inverse, contract_rows(rows_inverse, flat[...]))
        visitor = shift_box(arrived[match_index], [-value for value in outward])
        term = (potential * visitor).astype(jnp.bfloat16).astype(jnp.float32)
        term = jnp.where(live > 0, term, 0.0)
        total = term if total is None else total + term
    out_ref[...] = (-total).astype(out_ref.dtype)
    for started in copies:
        for copy in started:
            copy.wait_send()


def per_device(orbitals, pair_mask, offsets):
    extent, cells = orbitals.shape[1:]
    levels = lax.axis_size("orb").bit_length() - 1
    matches = pair_mask.shape[0]
    strides = [1 << match_index * (levels - 1) // (matches - 1) for match_index in range(matches)]
    pieces = cells // math.lcm(extent, LANES)
    operands = (offsets, pair_mask, *map(jnp.asarray, tables(extent)))
    spaces = [pltpu.SMEM] * 2 + [pltpu.VMEM] * (len(operands) - 2)
    exchange = pl.pallas_call(
        functools.partial(kernel, strides, pieces),
        out_shape=jax.ShapeDtypeStruct((extent, cells), jnp.bfloat16),
        in_specs=[pl.BlockSpec(memory_space=pltpu.HBM)] * (1 + len(operands)),
        out_specs=pl.BlockSpec(memory_space=pltpu.VMEM),
        scratch_shapes=[space(one.shape, one.dtype) for space, one in zip(spaces, operands)]
        + [
            pltpu.VMEM((extent, cells), jnp.bfloat16),
            pltpu.VMEM((matches, extent, cells), jnp.bfloat16),
            pltpu.VMEM((cells, LANES), jnp.float32),
            pltpu.VMEM((cells, LANES), jnp.float32),
            pltpu.VMEM((extent, cells), jnp.float32),
            pltpu.VMEM((extent, extent * LANES), jnp.float32),
            pltpu.VMEM((extent, cells), jnp.float32),
            pltpu.SemaphoreType.DMA((1 + len(operands),)),
            pltpu.SemaphoreType.DMA((matches, pieces)),
            pltpu.SemaphoreType.DMA((matches, pieces)),
        ],
        compiler_params=pltpu.CompilerParams(
            collective_id=0, has_side_effects=True, vmem_limit_bytes=64 * 1024 * 1024
        ),
        name="exchange",
    )(orbitals.reshape(extent, cells), *operands)
    return exchange.reshape(1, extent, cells)


def solution(mesh):
    placed = (P("orb", None, None), P(), P())
    return jax.shard_map(
        per_device, mesh=mesh, in_specs=placed, out_specs=P("orb", None, None), check_vma=False
    )
```

```python
import functools
import math

import jax
import jax.numpy as jnp
import ml_dtypes
import numpy as np
from jax import lax
from jax.experimental import pallas as pl
from jax.experimental.pallas import tpu as pltpu
from jax.sharding import PartitionSpec as P

screening = 0.5
MESH = pl.DeviceIdType.MESH
LANES = 128


def split(values):
    high = values.astype(jnp.bfloat16)
    low = (values - high.astype(jnp.float32)).astype(jnp.bfloat16)
    return high, low


def split_constant(values):
    high = values.astype(ml_dtypes.bfloat16)
    low = (values - high.astype(np.float64)).astype(ml_dtypes.bfloat16)
    return high, low


def tables(extent):
    modes = np.arange(1, extent + 1, dtype=np.float64)
    sines = math.sqrt(2.0 / (extent + 1)) * np.sin(
        math.pi * modes[:, None] * modes[None, :] / (extent + 1)
    )
    eigenvalue = 2.0 - 2.0 * np.cos(math.pi * modes / (extent + 1))
    padded = np.zeros((LANES, LANES))
    padded[:extent, :extent] = sines
    last = np.zeros(LANES)
    last[:extent] = eigenvalue
    eigen_lane = (eigenvalue[:, None] + last[None, :] + screening).reshape(1, extent * LANES)
    eigen_row = np.broadcast_to(eigenvalue[:, None], (extent, LANES))
    lane = np.arange(extent * extent)
    places = np.stack([lane // extent, lane % extent]).astype(np.int32)
    return (
        *split_constant(sines),
        *split_constant(padded),
        eigen_row.astype(np.float32),
        eigen_lane.astype(np.float32),
        places,
    )


def kernel(
    strides,
    pieces,
    orbital_ref,
    *refs,
):
    count = (len(refs) - 11) // 2
    sources, out_ref, held = refs[:count], refs[count], refs[count + 1 : 2 * count + 1]
    own, arrived, rows_in, rows_out, flat, symbol, moved_own, load_sem, send_sem, recv_sem = refs[
        2 * count + 1 :
    ]
    offsets_ref, mask_ref, sines_high_ref, sines_low_ref, padded_high_ref, padded_low_ref = held[:6]
    eigen_row_ref, eigen_lane_ref, places_ref = held[6:]
    extent, cells = own.shape
    width = math.lcm(extent, LANES)
    pieces = cells // width
    myself = lax.axis_index("orb")
    lows = [lax.rem(myself // stride, 2) == 0 for stride in strides]
    partners = [
        jnp.where(low, myself + stride, myself - stride) for low, stride in zip(lows, strides)
    ]

    loads = [
        pltpu.make_async_copy(source, target, load_sem.at[at])
        for at, (source, target) in enumerate(zip((orbital_ref, *sources), (own, *held)))
    ]
    barrier = pltpu.get_barrier_semaphore()
    for partner in partners:
        pl.semaphore_signal(barrier, inc=1, device_id={"orb": partner}, device_id_type=MESH)
    for load in loads:
        load.start()
    pl.semaphore_wait(barrier, len(strides))
    copies = [[] for _ in strides]
    for match_index in sorted(range(len(strides)), key=lambda at: -strides[at]):
        for piece in range(pieces):
            span = pl.ds(piece * width, width)
            copy = pltpu.make_async_remote_copy(
                src_ref=orbital_ref.at[:, span],
                dst_ref=arrived.at[match_index, :, span],
                send_sem=send_sem.at[match_index, piece],
                recv_sem=recv_sem.at[match_index, piece],
                device_id={"orb": partners[match_index]},
                device_id_type=MESH,
            )
            copy.start()
            copies[match_index].append(copy)
    for load in loads:
        load.wait()

    symbol[...] = 1.0 / (eigen_row_ref[:, :1] + eigen_lane_ref[...])
    per_width = width // extent

    def product(left, right):
        return jnp.dot(left, right, preferred_element_type=jnp.float32)

    def side_by_side(high, low):
        return jnp.concatenate([high, low, high], axis=1).astype(jnp.bfloat16)

    row = lax.broadcasted_iota(jnp.int32, (extent, extent), 0)
    column = lax.broadcasted_iota(jnp.int32, (extent, extent), 1)
    tile_row = lax.broadcasted_iota(jnp.int32, (LANES, LANES), 0)
    tile_column = lax.broadcasted_iota(jnp.int32, (LANES, LANES), 1)

    def forward_table(amount):
        pick = jnp.where(row - column == amount, 1.0, 0.0).astype(jnp.bfloat16)
        return side_by_side(product(sines_high_ref[...], pick), product(sines_low_ref[...], pick))

    def inverse_table(amount):
        pick = jnp.where(column - row == amount, 1.0, 0.0).astype(jnp.bfloat16)
        return side_by_side(product(pick, sines_high_ref[...]), product(pick, sines_low_ref[...]))

    def lane_table(high, low):
        high, low = high.astype(jnp.bfloat16), low.astype(jnp.bfloat16)
        upper = jnp.concatenate([high, low], axis=1)
        return jnp.concatenate([upper, jnp.concatenate([high, jnp.zeros_like(low)], axis=1)], axis=0)

    def forward_lanes(amount):
        pick = (tile_column - tile_row == amount) & (tile_row < extent)
        pick = jnp.where(pick, 1.0, 0.0).astype(jnp.bfloat16)
        return lane_table(product(pick, padded_high_ref[...]), product(pick, padded_low_ref[...]))

    def inverse_lanes(amount):
        pick = (tile_row - tile_column == amount) & (tile_column < extent)
        pick = jnp.where(pick, 1.0, 0.0).astype(jnp.bfloat16)
        return lane_table(product(padded_high_ref[...], pick), product(padded_low_ref[...], pick))

    def contract_rows(table, volume):
        high, low = split(volume)
        return product(table, jnp.concatenate([high, high, low], axis=0))

    def contract_lanes(table, volume):
        both = product(jnp.concatenate(split(volume), axis=1), table)
        return both[:, :LANES] + both[:, LANES:]

    def shift_box(volume, offset):
        pick = jnp.where(row - column == offset[0], 1.0, 0.0).astype(jnp.bfloat16)
        moved = product(pick, volume)
        turn = offset[1] * extent + offset[2]
        moved = pltpu.roll(moved, jnp.where(turn < 0, turn + cells, turn), 1)
        middle = places_ref[0:1, :] - offset[1]
        minor = places_ref[1:2, :] - offset[2]
        inside = (middle >= 0) & (middle < extent) & (minor >= 0) & (minor < extent)
        return jnp.where(inside, moved, 0.0)

    total = None
    for match_index, stride in enumerate(strides):
        is_low = lows[match_index]
        lower = jnp.where(is_low, myself, myself - stride)
        live = mask_ref[match_index, lower]
        offset = [offsets_ref[axis, match_index, lower] for axis in range(3)]
        ahead = [jnp.where(is_low, value, 0) for value in offset]
        behind = [jnp.where(is_low, 0, value) for value in offset]
        outward = [jnp.where(is_low, -value, value) for value in offset]
        moved_own[...] = shift_box(own[...], outward)
        rows_forward, middle_forward = forward_table(ahead[0]), forward_table(ahead[1])
        rows_inverse, middle_inverse = inverse_table(behind[0]), inverse_table(behind[1])
        lanes_forward, lanes_inverse = forward_lanes(ahead[2]), inverse_lanes(behind[2])

        for piece, copy in enumerate(copies[match_index]):
            copy.wait_recv()
            span = slice(piece * width, (piece + 1) * width)
            density = arrived[match_index, :, span].astype(jnp.float32) * moved_own[:, span]
            part = contract_rows(rows_forward, density)
            part = jnp.concatenate([part, part[:, :LANES]], axis=1)
            part = [part[:, at * extent : at * extent + LANES] for at in range(per_width)]
            part = contract_lanes(lanes_forward, jnp.concatenate(part, axis=0))
            for at in range(per_width):
                rows_in[pl.ds(piece * per_width + at, extent, stride=extent), :] = part[
                    at * extent : (at + 1) * extent
                ]
        volume = jnp.concatenate(
            [rows_in[at * extent : (at + 1) * extent, :] for at in range(extent)], axis=1
        )
        volume = symbol[...] * contract_rows(middle_forward, volume)
        volume = contract_rows(middle_inverse, volume)
        volume = jnp.concatenate(
            [volume[:, at * LANES : (at + 1) * LANES] for at in range(extent)], axis=0
        )
        rows_out[...] = contract_lanes(lanes_inverse, volume)
        for at in range(extent):
            flat[:, at * extent : (at + 1) * extent] = rows_out[
                pl.ds(at, extent, stride=extent), :
            ][:, :extent]
        potential = contract_rows(rows_inverse, flat[...])
        visitor = shift_box(arrived[match_index], [-value for value in outward])
        term = (potential * visitor).astype(jnp.bfloat16).astype(jnp.float32)
        term = jnp.where(live > 0, term, 0.0)
        total = term if total is None else total + term
    out_ref[...] = (-total).astype(out_ref.dtype)
    for started in copies:
        for copy in started:
            copy.wait_send()


def per_device(orbitals, pair_mask, offsets):
    extent, cells = orbitals.shape[1:]
    levels = lax.axis_size("orb").bit_length() - 1
    matches = pair_mask.shape[0]
    strides = [1 << match_index * (levels - 1) // (matches - 1) for match_index in range(matches)]
    pieces = cells // math.lcm(extent, LANES)
    operands = (offsets, pair_mask, *map(jnp.asarray, tables(extent)))
    spaces = [pltpu.SMEM] * 2 + [pltpu.VMEM] * (len(operands) - 2)
    exchange = pl.pallas_call(
        functools.partial(kernel, strides, pieces),
        out_shape=pltpu.VMEM((extent, cells), jnp.bfloat16),
        in_specs=[pl.BlockSpec(memory_space=pltpu.HBM)] * (1 + len(operands)),
        out_specs=pl.BlockSpec(memory_space=pltpu.VMEM),
        scratch_shapes=[space(one.shape, one.dtype) for space, one in zip(spaces, operands)]
        + [
            pltpu.VMEM((extent, cells), jnp.bfloat16),
            pltpu.VMEM((matches, extent, cells), jnp.bfloat16),
            pltpu.VMEM((cells, LANES), jnp.float32),
            pltpu.VMEM((cells, LANES), jnp.float32),
            pltpu.VMEM((extent, cells), jnp.float32),
            pltpu.VMEM((extent, extent * LANES), jnp.float32),
            pltpu.VMEM((extent, cells), jnp.float32),
            pltpu.SemaphoreType.DMA((1 + len(operands),)),
            pltpu.SemaphoreType.DMA((matches, pieces)),
            pltpu.SemaphoreType.DMA((matches, pieces)),
        ],
        compiler_params=pltpu.CompilerParams(
            collective_id=0, has_side_effects=True, vmem_limit_bytes=40 * 1024 * 1024
        ),
        name="exchange",
    )(*(pltpu.with_memory_space_constraint(one, pltpu.HBM) for one in (orbitals.reshape(extent, cells), *operands)))
    return exchange.reshape(1, extent, cells)


def solution(mesh):
    placed = (P("orb", None, None), P(), P())
    return jax.shard_map(
        per_device, mesh=mesh, in_specs=placed, out_specs=P("orb", None, None), check_vma=False
    )
```

```python
import functools
import math

import jax
import jax.numpy as jnp
import ml_dtypes
import numpy as np
from jax import lax
from jax.experimental import pallas as pl
from jax.experimental.pallas import tpu as pltpu
from jax.sharding import PartitionSpec as P

screening = 0.5
MESH = pl.DeviceIdType.MESH
LANES = 128


def split(values):
    high = values.astype(jnp.bfloat16)
    low = (values - high.astype(jnp.float32)).astype(jnp.bfloat16)
    return high, low


def split_constant(values):
    high = values.astype(ml_dtypes.bfloat16)
    low = (values - high.astype(np.float64)).astype(ml_dtypes.bfloat16)
    return high, low


def packed(extent):
    pack = LANES // extent
    while extent % (8 * pack):
        pack -= 1
    return pack


def tables(extent):
    modes = np.arange(1, extent + 1, dtype=np.float64)
    sines = math.sqrt(2.0 / (extent + 1)) * np.sin(
        math.pi * modes[:, None] * modes[None, :] / (extent + 1)
    )
    eigenvalue = 2.0 - 2.0 * np.cos(math.pi * modes / (extent + 1))
    pack = packed(extent)
    padded = np.zeros((LANES, LANES))
    padded[: pack * extent, : pack * extent] = np.kron(np.eye(pack), sines)
    tiles = extent // pack
    last = np.zeros((tiles, LANES))
    for at in range(pack):
        first = eigenvalue[at * tiles : (at + 1) * tiles]
        last[:, at * extent : (at + 1) * extent] = first[:, None] + eigenvalue[None, :]
    eigen_lane = (last + screening).reshape(1, tiles * LANES)
    eigen_row = np.broadcast_to(eigenvalue[:, None], (extent, LANES))
    lane = np.arange(extent * extent)
    places = np.stack([lane // extent, lane % extent]).astype(np.int32)
    return (
        *split_constant(sines),
        *split_constant(padded),
        eigen_row.astype(np.float32),
        eigen_lane.astype(np.float32),
        places,
    )


def kernel(
    strides,
    pieces,
    orbital_ref,
    *refs,
):
    count = (len(refs) - 11) // 2
    sources, out_ref, held = refs[:count], refs[count], refs[count + 1 : 2 * count + 1]
    own, arrived, rows_in, rows_out, flat, symbol, moved_own, load_sem, send_sem, recv_sem = refs[
        2 * count + 1 :
    ]
    offsets_ref, mask_ref, sines_high_ref, sines_low_ref, padded_high_ref, padded_low_ref = held[:6]
    eigen_row_ref, eigen_lane_ref, places_ref = held[6:]
    extent, cells = own.shape
    width = math.lcm(extent, LANES)
    pieces = cells // width
    pack = packed(extent)
    tiles = extent // pack
    myself = lax.axis_index("orb")
    lows = [lax.rem(myself // stride, 2) == 0 for stride in strides]
    partners = [
        jnp.where(low, myself + stride, myself - stride) for low, stride in zip(lows, strides)
    ]

    loads = [
        pltpu.make_async_copy(source, target, load_sem.at[at])
        for at, (source, target) in enumerate(zip((orbital_ref, *sources), (own, *held)))
    ]
    barrier = pltpu.get_barrier_semaphore()
    for partner in partners:
        pl.semaphore_signal(barrier, inc=1, device_id={"orb": partner}, device_id_type=MESH)
    for load in loads:
        load.start()
    pl.semaphore_wait(barrier, len(strides))
    copies = [[] for _ in strides]
    for match_index in sorted(range(len(strides)), key=lambda at: -strides[at]):
        for piece in range(pieces):
            span = pl.ds(piece * width, width)
            copy = pltpu.make_async_remote_copy(
                src_ref=orbital_ref.at[:, span],
                dst_ref=arrived.at[match_index, :, span],
                send_sem=send_sem.at[match_index, piece],
                recv_sem=recv_sem.at[match_index, piece],
                device_id={"orb": partners[match_index]},
                device_id_type=MESH,
            )
            copy.start()
            copies[match_index].append(copy)
    for load in loads:
        load.wait()

    symbol[...] = 1.0 / (eigen_row_ref[:, :1] + eigen_lane_ref[...])
    per_width = width // extent

    def product(left, right):
        return jnp.dot(left, right, preferred_element_type=jnp.float32)

    def side_by_side(high, low):
        return jnp.concatenate([high, low, high], axis=1).astype(jnp.bfloat16)

    row = lax.broadcasted_iota(jnp.int32, (extent, extent), 0)
    column = lax.broadcasted_iota(jnp.int32, (extent, extent), 1)
    tile_row = lax.broadcasted_iota(jnp.int32, (LANES, LANES), 0)
    tile_column = lax.broadcasted_iota(jnp.int32, (LANES, LANES), 1)
    tile_minor = places_ref[1:2, :LANES]
    tile_block = places_ref[0:1, :LANES]

    def forward_table(amount):
        pick = jnp.where(row - column == amount, 1.0, 0.0).astype(jnp.bfloat16)
        return side_by_side(product(sines_high_ref[...], pick), product(sines_low_ref[...], pick))

    def inverse_table(amount):
        pick = jnp.where(column - row == amount, 1.0, 0.0).astype(jnp.bfloat16)
        return side_by_side(product(pick, sines_high_ref[...]), product(pick, sines_low_ref[...]))

    def lane_table(high, low):
        high, low = high.astype(jnp.bfloat16), low.astype(jnp.bfloat16)
        upper = jnp.concatenate([high, low], axis=1)
        return jnp.concatenate([upper, jnp.concatenate([high, jnp.zeros_like(low)], axis=1)], axis=0)

    def forward_lanes(amount):
        inside = (tile_minor >= amount) & (tile_minor < extent + amount)
        pick = (tile_column - tile_row == amount) & inside
        pick = jnp.where(pick, 1.0, 0.0).astype(jnp.bfloat16)
        return lane_table(product(pick, padded_high_ref[...]), product(pick, padded_low_ref[...]))

    def inverse_lanes(amount):
        inside = (tile_minor >= -amount) & (tile_minor < extent - amount)
        pick = (tile_row - tile_column == amount) & inside
        pick = jnp.where(pick, 1.0, 0.0).astype(jnp.bfloat16)
        return lane_table(product(padded_high_ref[...], pick), product(padded_low_ref[...], pick))

    def contract_rows(table, volume):
        high, low = split(volume)
        return product(table, jnp.concatenate([high, high, low], axis=0))

    def contract_lanes(table, volume):
        both = product(jnp.concatenate(split(volume), axis=1), table)
        return both[:, :LANES] + both[:, LANES:]

    def shift_box(volume, offset):
        pick = jnp.where(row - column == offset[0], 1.0, 0.0).astype(jnp.bfloat16)
        moved = product(pick, volume)
        turn = offset[1] * extent + offset[2]
        moved = pltpu.roll(moved, jnp.where(turn < 0, turn + cells, turn), 1)
        middle = places_ref[0:1, :] - offset[1]
        minor = places_ref[1:2, :] - offset[2]
        inside = (middle >= 0) & (middle < extent) & (minor >= 0) & (minor < extent)
        return jnp.where(inside, moved, 0.0)

    total = None
    for match_index, stride in enumerate(strides):
        is_low = lows[match_index]
        lower = jnp.where(is_low, myself, myself - stride)
        live = mask_ref[match_index, lower]
        offset = [offsets_ref[axis, match_index, lower] for axis in range(3)]
        ahead = [jnp.where(is_low, value, 0) for value in offset]
        behind = [jnp.where(is_low, 0, value) for value in offset]
        outward = [jnp.where(is_low, -value, value) for value in offset]
        moved_own[...] = shift_box(own[...], outward)
        rows_forward, middle_forward = forward_table(ahead[0]), forward_table(ahead[1])
        rows_inverse, middle_inverse = inverse_table(behind[0]), inverse_table(behind[1])
        lanes_forward, lanes_inverse = forward_lanes(ahead[2]), inverse_lanes(behind[2])

        for piece, copy in enumerate(copies[match_index]):
            copy.wait_recv()
            span = slice(piece * width, (piece + 1) * width)
            density = arrived[match_index, :, span].astype(jnp.float32) * moved_own[:, span]
            part = contract_rows(rows_forward, density)
            part = jnp.concatenate([part[:, -LANES:], part, part[:, :LANES]], axis=1)
            slabs = []
            for at in range(per_width):
                slab = None
                for lap in range(pack):
                    start = LANES + (at - lap) * extent
                    window = part[lap * tiles : (lap + 1) * tiles, start : start + LANES]
                    slab = window if slab is None else jnp.where(tile_block < lap, slab, window)
                slabs.append(slab)
            part = contract_lanes(lanes_forward, jnp.concatenate(slabs, axis=0))
            for at in range(per_width):
                rows_in[pl.ds(piece * per_width + at, tiles, stride=extent), :] = part[
                    at * tiles : (at + 1) * tiles
                ]
        volume = jnp.concatenate(
            [rows_in[at * extent : (at + 1) * extent, :] for at in range(tiles)], axis=1
        )
        volume = symbol[...] * contract_rows(middle_forward, volume)
        volume = contract_rows(middle_inverse, volume)
        volume = jnp.concatenate(
            [volume[:, at * LANES : (at + 1) * LANES] for at in range(tiles)], axis=0
        )
        rows_out[...] = contract_lanes(lanes_inverse, volume)
        for at in range(extent):
            slab = rows_out[pl.ds(at, tiles, stride=extent), :]
            for lap in range(pack):
                flat[lap * tiles : (lap + 1) * tiles, at * extent : (at + 1) * extent] = slab[
                    :, lap * extent : (lap + 1) * extent
                ]
        potential = contract_rows(rows_inverse, flat[...])
        visitor = shift_box(arrived[match_index], [-value for value in outward])
        term = (potential * visitor).astype(jnp.bfloat16).astype(jnp.float32)
        term = jnp.where(live > 0, term, 0.0)
        total = term if total is None else total + term
    out_ref[...] = (-total).astype(out_ref.dtype)
    for started in copies:
        for copy in started:
            copy.wait_send()


def per_device(orbitals, pair_mask, offsets):
    extent, cells = orbitals.shape[1:]
    levels = lax.axis_size("orb").bit_length() - 1
    matches = pair_mask.shape[0]
    strides = [1 << match_index * (levels - 1) // (matches - 1) for match_index in range(matches)]
    pieces = cells // math.lcm(extent, LANES)
    operands = (offsets, pair_mask, *map(jnp.asarray, tables(extent)))
    spaces = [pltpu.SMEM] * 2 + [pltpu.VMEM] * (len(operands) - 2)
    exchange = pl.pallas_call(
        functools.partial(kernel, strides, pieces),
        out_shape=pltpu.VMEM((extent, cells), jnp.bfloat16),
        in_specs=[pl.BlockSpec(memory_space=pltpu.HBM)] * (1 + len(operands)),
        out_specs=pl.BlockSpec(memory_space=pltpu.VMEM),
        scratch_shapes=[space(one.shape, one.dtype) for space, one in zip(spaces, operands)]
        + [
            pltpu.VMEM((extent, cells), jnp.bfloat16),
            pltpu.VMEM((matches, extent, cells), jnp.bfloat16),
            pltpu.VMEM((cells // packed(extent), LANES), jnp.float32),
            pltpu.VMEM((cells // packed(extent), LANES), jnp.float32),
            pltpu.VMEM((extent, cells), jnp.float32),
            pltpu.VMEM((extent, extent // packed(extent) * LANES), jnp.float32),
            pltpu.VMEM((extent, cells), jnp.float32),
            pltpu.SemaphoreType.DMA((1 + len(operands),)),
            pltpu.SemaphoreType.DMA((matches, pieces)),
            pltpu.SemaphoreType.DMA((matches, pieces)),
        ],
        compiler_params=pltpu.CompilerParams(
            collective_id=0, has_side_effects=True, vmem_limit_bytes=40 * 1024 * 1024
        ),
        name="exchange",
    )(*(pltpu.with_memory_space_constraint(one, pltpu.HBM) for one in (orbitals.reshape(extent, cells), *operands)))
    return exchange.reshape(1, extent, cells)


def solution(mesh):
    placed = (P("orb", None, None), P(), P())
    return jax.shard_map(
        per_device, mesh=mesh, in_specs=placed, out_specs=P("orb", None, None), check_vma=False
    )
```

```python
import functools
import math

import jax
import jax.numpy as jnp
import ml_dtypes
import numpy as np
from jax import lax
from jax.experimental import pallas as pl
from jax.experimental.pallas import tpu as pltpu
from jax.sharding import PartitionSpec as P

screening = 0.5
MESH = pl.DeviceIdType.MESH
LANES = 128


def split(values):
    high = values.astype(jnp.bfloat16)
    low = (values - high.astype(jnp.float32)).astype(jnp.bfloat16)
    return high, low


def split_constant(values):
    high = values.astype(ml_dtypes.bfloat16)
    low = (values - high.astype(np.float64)).astype(ml_dtypes.bfloat16)
    return high, low


def packed(extent):
    pack = LANES // extent
    while extent % (8 * pack):
        pack -= 1
    return pack


def tables(extent):
    modes = np.arange(1, extent + 1, dtype=np.float64)
    sines = math.sqrt(2.0 / (extent + 1)) * np.sin(
        math.pi * modes[:, None] * modes[None, :] / (extent + 1)
    )
    eigenvalue = 2.0 - 2.0 * np.cos(math.pi * modes / (extent + 1))
    pack = packed(extent)
    padded = np.zeros((LANES, LANES))
    padded[: pack * extent, : pack * extent] = np.kron(np.eye(pack), sines)
    tiles = extent // pack
    last = np.zeros((tiles, LANES))
    for at in range(pack):
        first = eigenvalue[at * tiles : (at + 1) * tiles]
        last[:, at * extent : (at + 1) * extent] = first[:, None] + eigenvalue[None, :]
    eigen_lane = (last + screening).reshape(1, tiles * LANES)
    eigen_row = np.broadcast_to(eigenvalue[:, None], (extent, LANES))
    lane = np.arange(extent * extent)
    places = np.stack([lane // extent, lane % extent]).astype(np.int32)
    return (
        *split_constant(sines),
        *split_constant(padded),
        eigen_row.astype(np.float32),
        eigen_lane.astype(np.float32),
        places,
    )


def kernel(
    strides,
    pieces,
    orbital_ref,
    *refs,
):
    count = (len(refs) - 11) // 2
    sources, out_ref, held = refs[:count], refs[count], refs[count + 1 : 2 * count + 1]
    own, arrived, rows_in, rows_out, flat, symbol, moved_own, load_sem, send_sem, recv_sem = refs[
        2 * count + 1 :
    ]
    offsets_ref, mask_ref, sines_high_ref, sines_low_ref, padded_high_ref, padded_low_ref = held[:6]
    eigen_row_ref, eigen_lane_ref, places_ref = held[6:]
    extent, cells = own.shape
    width = math.lcm(extent, LANES)
    pieces = cells // width
    pack = packed(extent)
    tiles = extent // pack
    myself = lax.axis_index("orb")
    lows = [lax.rem(myself // stride, 2) == 0 for stride in strides]
    partners = [
        jnp.where(low, myself + stride, myself - stride) for low, stride in zip(lows, strides)
    ]

    loads = [
        pltpu.make_async_copy(source, target, load_sem.at[at])
        for at, (source, target) in enumerate(zip((orbital_ref, *sources), (own, *held)))
    ]
    barrier = pltpu.get_barrier_semaphore()
    for partner in partners:
        pl.semaphore_signal(barrier, inc=1, device_id={"orb": partner}, device_id_type=MESH)
    for load in loads:
        load.start()
    pl.semaphore_wait(barrier, len(strides))
    copies = [
        [
            pltpu.make_async_remote_copy(
                src_ref=orbital_ref.at[:, pl.ds(piece * width, width)],
                dst_ref=arrived.at[match_index, :, pl.ds(piece * width, width)],
                send_sem=send_sem.at[match_index, piece],
                recv_sem=recv_sem.at[match_index, piece],
                device_id={"orb": partners[match_index]},
                device_id_type=MESH,
            )
            for piece in range(pieces)
        ]
        for match_index in range(len(strides))
    ]
    far = len(strides) - 1
    yields = lax.rem(myself // max(strides[far] // 2, 1), 4) == 3

    def send(match_index):
        for copy in copies[match_index]:
            copy.start()

    @pl.when(jnp.logical_not(yields))
    def _():
        send(far)

    for match_index in range(far):
        send(match_index)
    for load in loads:
        load.wait()

    symbol[...] = 1.0 / (eigen_row_ref[:, :1] + eigen_lane_ref[...])
    per_width = width // extent

    def product(left, right):
        return jnp.dot(left, right, preferred_element_type=jnp.float32)

    def side_by_side(high, low):
        return jnp.concatenate([high, low, high], axis=1).astype(jnp.bfloat16)

    row = lax.broadcasted_iota(jnp.int32, (extent, extent), 0)
    column = lax.broadcasted_iota(jnp.int32, (extent, extent), 1)
    tile_row = lax.broadcasted_iota(jnp.int32, (LANES, LANES), 0)
    tile_column = lax.broadcasted_iota(jnp.int32, (LANES, LANES), 1)
    tile_minor = places_ref[1:2, :LANES]
    tile_block = places_ref[0:1, :LANES]

    def forward_table(amount):
        pick = jnp.where(row - column == amount, 1.0, 0.0).astype(jnp.bfloat16)
        return side_by_side(product(sines_high_ref[...], pick), product(sines_low_ref[...], pick))

    def inverse_table(amount):
        pick = jnp.where(column - row == amount, 1.0, 0.0).astype(jnp.bfloat16)
        return side_by_side(product(pick, sines_high_ref[...]), product(pick, sines_low_ref[...]))

    def lane_table(high, low):
        high, low = high.astype(jnp.bfloat16), low.astype(jnp.bfloat16)
        upper = jnp.concatenate([high, low], axis=1)
        return jnp.concatenate([upper, jnp.concatenate([high, jnp.zeros_like(low)], axis=1)], axis=0)

    def forward_lanes(amount):
        inside = (tile_minor >= amount) & (tile_minor < extent + amount)
        pick = (tile_column - tile_row == amount) & inside
        pick = jnp.where(pick, 1.0, 0.0).astype(jnp.bfloat16)
        return lane_table(product(pick, padded_high_ref[...]), product(pick, padded_low_ref[...]))

    def inverse_lanes(amount):
        inside = (tile_minor >= -amount) & (tile_minor < extent - amount)
        pick = (tile_row - tile_column == amount) & inside
        pick = jnp.where(pick, 1.0, 0.0).astype(jnp.bfloat16)
        return lane_table(product(padded_high_ref[...], pick), product(padded_low_ref[...], pick))

    def contract_rows(table, volume):
        high, low = split(volume)
        return product(table, jnp.concatenate([high, high, low], axis=0))

    def contract_lanes(table, volume):
        both = product(jnp.concatenate(split(volume), axis=1), table)
        return both[:, :LANES] + both[:, LANES:]

    def shift_box(volume, offset):
        pick = jnp.where(row - column == offset[0], 1.0, 0.0).astype(jnp.bfloat16)
        moved = product(pick, volume)
        turn = offset[1] * extent + offset[2]
        moved = pltpu.roll(moved, jnp.where(turn < 0, turn + cells, turn), 1)
        middle = places_ref[0:1, :] - offset[1]
        minor = places_ref[1:2, :] - offset[2]
        inside = (middle >= 0) & (middle < extent) & (minor >= 0) & (minor < extent)
        return jnp.where(inside, moved, 0.0)

    total = None
    for match_index, stride in enumerate(strides):
        is_low = lows[match_index]
        lower = jnp.where(is_low, myself, myself - stride)
        live = mask_ref[match_index, lower]
        offset = [offsets_ref[axis, match_index, lower] for axis in range(3)]
        ahead = [jnp.where(is_low, value, 0) for value in offset]
        behind = [jnp.where(is_low, 0, value) for value in offset]
        outward = [jnp.where(is_low, -value, value) for value in offset]
        moved_own[...] = shift_box(own[...], outward)
        rows_forward, middle_forward = forward_table(ahead[0]), forward_table(ahead[1])
        rows_inverse, middle_inverse = inverse_table(behind[0]), inverse_table(behind[1])
        lanes_forward, lanes_inverse = forward_lanes(ahead[2]), inverse_lanes(behind[2])

        if match_index == min(1, far):

            @pl.when(yields)
            def _():
                send(far)

        for piece, copy in enumerate(copies[match_index]):
            copy.wait_recv()
            span = slice(piece * width, (piece + 1) * width)
            density = arrived[match_index, :, span].astype(jnp.float32) * moved_own[:, span]
            part = contract_rows(rows_forward, density)
            part = jnp.concatenate([part[:, -LANES:], part, part[:, :LANES]], axis=1)
            slabs = []
            for at in range(per_width):
                slab = None
                for lap in range(pack):
                    start = LANES + (at - lap) * extent
                    window = part[lap * tiles : (lap + 1) * tiles, start : start + LANES]
                    slab = window if slab is None else jnp.where(tile_block < lap, slab, window)
                slabs.append(slab)
            part = contract_lanes(lanes_forward, jnp.concatenate(slabs, axis=0))
            for at in range(per_width):
                rows_in[pl.ds(piece * per_width + at, tiles, stride=extent), :] = part[
                    at * tiles : (at + 1) * tiles
                ]
        volume = jnp.concatenate(
            [rows_in[at * extent : (at + 1) * extent, :] for at in range(tiles)], axis=1
        )
        volume = symbol[...] * contract_rows(middle_forward, volume)
        volume = contract_rows(middle_inverse, volume)
        volume = jnp.concatenate(
            [volume[:, at * LANES : (at + 1) * LANES] for at in range(tiles)], axis=0
        )
        rows_out[...] = contract_lanes(lanes_inverse, volume)
        for at in range(extent):
            slab = rows_out[pl.ds(at, tiles, stride=extent), :]
            for lap in range(pack):
                flat[lap * tiles : (lap + 1) * tiles, at * extent : (at + 1) * extent] = slab[
                    :, lap * extent : (lap + 1) * extent
                ]
        potential = contract_rows(rows_inverse, flat[...])
        visitor = shift_box(arrived[match_index], [-value for value in outward])
        term = (potential * visitor).astype(jnp.bfloat16).astype(jnp.float32)
        term = jnp.where(live > 0, term, 0.0)
        total = term if total is None else total + term
    out_ref[...] = (-total).astype(out_ref.dtype)
    for started in copies:
        for copy in started:
            copy.wait_send()


def per_device(orbitals, pair_mask, offsets):
    extent, cells = orbitals.shape[1:]
    levels = lax.axis_size("orb").bit_length() - 1
    matches = pair_mask.shape[0]
    strides = [1 << match_index * (levels - 1) // (matches - 1) for match_index in range(matches)]
    pieces = cells // math.lcm(extent, LANES)
    operands = (offsets, pair_mask, *map(jnp.asarray, tables(extent)))
    spaces = [pltpu.SMEM] * 2 + [pltpu.VMEM] * (len(operands) - 2)
    exchange = pl.pallas_call(
        functools.partial(kernel, strides, pieces),
        out_shape=pltpu.VMEM((extent, cells), jnp.bfloat16),
        in_specs=[pl.BlockSpec(memory_space=pltpu.HBM)] * (1 + len(operands)),
        out_specs=pl.BlockSpec(memory_space=pltpu.VMEM),
        scratch_shapes=[space(one.shape, one.dtype) for space, one in zip(spaces, operands)]
        + [
            pltpu.VMEM((extent, cells), jnp.bfloat16),
            pltpu.VMEM((matches, extent, cells), jnp.bfloat16),
            pltpu.VMEM((cells // packed(extent), LANES), jnp.float32),
            pltpu.VMEM((cells // packed(extent), LANES), jnp.float32),
            pltpu.VMEM((extent, cells), jnp.float32),
            pltpu.VMEM((extent, extent // packed(extent) * LANES), jnp.float32),
            pltpu.VMEM((extent, cells), jnp.float32),
            pltpu.SemaphoreType.DMA((1 + len(operands),)),
            pltpu.SemaphoreType.DMA((matches, pieces)),
            pltpu.SemaphoreType.DMA((matches, pieces)),
        ],
        compiler_params=pltpu.CompilerParams(
            collective_id=0, has_side_effects=True, vmem_limit_bytes=40 * 1024 * 1024
        ),
        name="exchange",
    )(*(pltpu.with_memory_space_constraint(one, pltpu.HBM) for one in (orbitals.reshape(extent, cells), *operands)))
    return exchange.reshape(1, extent, cells)


def solution(mesh):
    placed = (P("orb", None, None), P(), P())
    return jax.shard_map(
        per_device, mesh=mesh, in_specs=placed, out_specs=P("orb", None, None), check_vma=False
    )
```

```python
import functools
import math

import jax
import jax.numpy as jnp
import ml_dtypes
import numpy as np
from jax import lax
from jax.experimental import pallas as pl
from jax.experimental.pallas import tpu as pltpu
from jax.sharding import PartitionSpec as P

screening = 0.5
MESH = pl.DeviceIdType.MESH
LANES = 128


def split(values):
    high = values.astype(jnp.bfloat16)
    low = (values - high.astype(jnp.float32)).astype(jnp.bfloat16)
    return high, low


def split_constant(values):
    high = values.astype(ml_dtypes.bfloat16)
    low = (values - high.astype(np.float64)).astype(ml_dtypes.bfloat16)
    return high, low


def packed(extent):
    pack = LANES // extent
    while extent % (8 * pack):
        pack -= 1
    return pack


def tables(extent):
    modes = np.arange(1, extent + 1, dtype=np.float64)
    sines = math.sqrt(2.0 / (extent + 1)) * np.sin(
        math.pi * modes[:, None] * modes[None, :] / (extent + 1)
    )
    eigenvalue = 2.0 - 2.0 * np.cos(math.pi * modes / (extent + 1))
    pack = packed(extent)
    padded = np.zeros((LANES, LANES))
    padded[: pack * extent, : pack * extent] = np.kron(np.eye(pack), sines)
    tiles = extent // pack
    last = np.zeros((tiles, LANES))
    for at in range(pack):
        first = eigenvalue[at * tiles : (at + 1) * tiles]
        last[:, at * extent : (at + 1) * extent] = first[:, None] + eigenvalue[None, :]
    eigen_lane = (last + screening).reshape(1, tiles * LANES)
    eigen_row = np.broadcast_to(eigenvalue[:, None], (extent, LANES))
    lane = np.arange(extent * extent)
    places = np.stack([lane // extent, lane % extent]).astype(np.int32)
    return (
        *split_constant(sines),
        *split_constant(padded),
        eigen_row.astype(np.float32),
        eigen_lane.astype(np.float32),
        places,
    )


def kernel(
    strides,
    pieces,
    orbital_ref,
    *refs,
):
    count = (len(refs) - 12) // 2
    sources, out_ref, held = refs[:count], refs[count], refs[count + 1 : 2 * count + 1]
    own, arrived, rows_in, rows_out, flat, symbol, moved_own, moved_theirs, load_sem, send_sem, recv_sem = refs[
        2 * count + 1 :
    ]
    offsets_ref, mask_ref, sines_high_ref, sines_low_ref, padded_high_ref, padded_low_ref = held[:6]
    eigen_row_ref, eigen_lane_ref, places_ref = held[6:]
    extent, cells = own.shape
    width = math.lcm(extent, LANES)
    pieces = cells // width
    pack = packed(extent)
    tiles = extent // pack
    myself = lax.axis_index("orb")
    lows = [lax.rem(myself // stride, 2) == 0 for stride in strides]
    partners = [
        jnp.where(low, myself + stride, myself - stride) for low, stride in zip(lows, strides)
    ]

    loads = [
        pltpu.make_async_copy(source, target, load_sem.at[at])
        for at, (source, target) in enumerate(zip((orbital_ref, *sources), (own, *held)))
    ]
    barrier = pltpu.get_barrier_semaphore()
    for partner in partners:
        pl.semaphore_signal(barrier, inc=1, device_id={"orb": partner}, device_id_type=MESH)
    for load in loads:
        load.start()
    pl.semaphore_wait(barrier, len(strides))
    copies = [
        [
            pltpu.make_async_remote_copy(
                src_ref=orbital_ref.at[:, pl.ds(piece * width, width)],
                dst_ref=arrived.at[match_index, :, pl.ds(piece * width, width)],
                send_sem=send_sem.at[match_index, piece],
                recv_sem=recv_sem.at[match_index, piece],
                device_id={"orb": partners[match_index]},
                device_id_type=MESH,
            )
            for piece in range(pieces)
        ]
        for match_index in range(len(strides))
    ]
    far = len(strides) - 1
    early = pieces // 3
    yields = lax.rem(myself // max(strides[far] // 2, 1), 4) == 3

    def send(match_index, part=slice(None)):
        for copy in copies[match_index][part]:
            copy.start()

    @pl.when(jnp.logical_not(yields))
    def _():
        send(far)

    for match_index in range(far):
        send(match_index)
    for load in loads:
        load.wait()

    symbol[...] = 1.0 / (eigen_row_ref[:, :1] + eigen_lane_ref[...])
    per_width = width // extent

    def product(left, right):
        return jnp.dot(left, right, preferred_element_type=jnp.float32)

    def side_by_side(high, low):
        return jnp.concatenate([high, low, high], axis=1).astype(jnp.bfloat16)

    row = lax.broadcasted_iota(jnp.int32, (extent, extent), 0)
    column = lax.broadcasted_iota(jnp.int32, (extent, extent), 1)
    tile_row = lax.broadcasted_iota(jnp.int32, (LANES, LANES), 0)
    tile_column = lax.broadcasted_iota(jnp.int32, (LANES, LANES), 1)
    tile_minor = places_ref[1:2, :LANES]
    tile_block = places_ref[0:1, :LANES]

    def forward_table(amount):
        pick = jnp.where(row - column == amount, 1.0, 0.0).astype(jnp.bfloat16)
        return side_by_side(product(sines_high_ref[...], pick), product(sines_low_ref[...], pick))

    def inverse_table(amount):
        pick = jnp.where(column - row == amount, 1.0, 0.0).astype(jnp.bfloat16)
        return side_by_side(product(pick, sines_high_ref[...]), product(pick, sines_low_ref[...]))

    def lane_table(high, low):
        high, low = high.astype(jnp.bfloat16), low.astype(jnp.bfloat16)
        upper = jnp.concatenate([high, low], axis=1)
        return jnp.concatenate([upper, jnp.concatenate([high, jnp.zeros_like(low)], axis=1)], axis=0)

    def forward_lanes(amount):
        inside = (tile_minor >= amount) & (tile_minor < extent + amount)
        pick = (tile_column - tile_row == amount) & inside
        pick = jnp.where(pick, 1.0, 0.0).astype(jnp.bfloat16)
        return lane_table(product(pick, padded_high_ref[...]), product(pick, padded_low_ref[...]))

    def inverse_lanes(amount):
        inside = (tile_minor >= -amount) & (tile_minor < extent - amount)
        pick = (tile_row - tile_column == amount) & inside
        pick = jnp.where(pick, 1.0, 0.0).astype(jnp.bfloat16)
        return lane_table(product(padded_high_ref[...], pick), product(padded_low_ref[...], pick))

    def contract_rows(table, volume):
        high, low = split(volume)
        return product(table, jnp.concatenate([high, high, low], axis=0))

    def contract_lanes(table, volume):
        both = product(jnp.concatenate(split(volume), axis=1), table)
        return both[:, :LANES] + both[:, LANES:]

    def shift_rows(volume, amount):
        pick = jnp.where(row - column == amount, 1.0, 0.0).astype(jnp.bfloat16)
        return product(pick, volume)

    def shift_lanes(moved, offset):
        turn = offset[1] * extent + offset[2]
        moved = pltpu.roll(moved, jnp.where(turn < 0, turn + cells, turn), 1)
        middle = places_ref[0:1, :] - offset[1]
        minor = places_ref[1:2, :] - offset[2]
        inside = (middle >= 0) & (middle < extent) & (minor >= 0) & (minor < extent)
        return jnp.where(inside, moved, 0.0)

    total = None
    for match_index, stride in enumerate(strides):
        is_low = lows[match_index]
        lower = jnp.where(is_low, myself, myself - stride)
        live = mask_ref[match_index, lower]
        offset = [offsets_ref[axis, match_index, lower] for axis in range(3)]
        ahead = [jnp.where(is_low, value, 0) for value in offset]
        behind = [jnp.where(is_low, 0, value) for value in offset]
        outward = [jnp.where(is_low, -value, value) for value in offset]
        inward = [-value for value in outward]
        moved_own[...] = shift_lanes(shift_rows(own[...], outward[0]), outward)
        rows_forward, middle_forward = forward_table(ahead[0]), forward_table(ahead[1])
        rows_inverse, middle_inverse = inverse_table(behind[0]), inverse_table(behind[1])
        lanes_forward, lanes_inverse = forward_lanes(ahead[2]), inverse_lanes(behind[2])

        if match_index == min(1, far):

            @pl.when(yields)
            def _():
                send(far, slice(early if far else 0, None))

        for piece, copy in enumerate(copies[match_index]):
            copy.wait_recv()
            span = slice(piece * width, (piece + 1) * width)
            theirs = arrived[match_index, :, span]
            moved_theirs[:, span] = shift_rows(theirs, inward[0])
            density = theirs.astype(jnp.float32) * moved_own[:, span]
            part = contract_rows(rows_forward, density)
            part = jnp.concatenate([part[:, -LANES:], part, part[:, :LANES]], axis=1)
            slabs = []
            for at in range(per_width):
                slab = None
                for lap in range(pack):
                    start = LANES + (at - lap) * extent
                    window = part[lap * tiles : (lap + 1) * tiles, start : start + LANES]
                    slab = window if slab is None else jnp.where(tile_block < lap, slab, window)
                slabs.append(slab)
            part = contract_lanes(lanes_forward, jnp.concatenate(slabs, axis=0))
            for at in range(per_width):
                rows_in[pl.ds(piece * per_width + at, tiles, stride=extent), :] = part[
                    at * tiles : (at + 1) * tiles
                ]
        if match_index < min(1, far):

            @pl.when(yields)
            def _():
                send(far, slice(early))

        volume = jnp.concatenate(
            [rows_in[at * extent : (at + 1) * extent, :] for at in range(tiles)], axis=1
        )
        volume = symbol[...] * contract_rows(middle_forward, volume)
        volume = contract_rows(middle_inverse, volume)
        volume = jnp.concatenate(
            [volume[:, at * LANES : (at + 1) * LANES] for at in range(tiles)], axis=0
        )
        rows_out[...] = contract_lanes(lanes_inverse, volume)
        for at in range(extent):
            slab = rows_out[pl.ds(at, tiles, stride=extent), :]
            for lap in range(pack):
                flat[lap * tiles : (lap + 1) * tiles, at * extent : (at + 1) * extent] = slab[
                    :, lap * extent : (lap + 1) * extent
                ]
        potential = contract_rows(rows_inverse, flat[...])
        visitor = shift_lanes(moved_theirs[...], inward)
        term = (potential * visitor).astype(jnp.bfloat16).astype(jnp.float32)
        term = jnp.where(live > 0, term, 0.0)
        total = term if total is None else total + term
    out_ref[...] = (-total).astype(out_ref.dtype)
    for started in copies:
        for copy in started:
            copy.wait_send()


def per_device(orbitals, pair_mask, offsets):
    extent, cells = orbitals.shape[1:]
    levels = lax.axis_size("orb").bit_length() - 1
    matches = pair_mask.shape[0]
    strides = [1 << match_index * (levels - 1) // (matches - 1) for match_index in range(matches)]
    pieces = cells // math.lcm(extent, LANES)
    operands = (offsets, pair_mask, *map(jnp.asarray, tables(extent)))
    spaces = [pltpu.SMEM] * 2 + [pltpu.VMEM] * (len(operands) - 2)
    exchange = pl.pallas_call(
        functools.partial(kernel, strides, pieces),
        out_shape=pltpu.VMEM((extent, cells), jnp.bfloat16),
        in_specs=[pl.BlockSpec(memory_space=pltpu.HBM)] * (1 + len(operands)),
        out_specs=pl.BlockSpec(memory_space=pltpu.VMEM),
        scratch_shapes=[space(one.shape, one.dtype) for space, one in zip(spaces, operands)]
        + [
            pltpu.VMEM((extent, cells), jnp.bfloat16),
            pltpu.VMEM((matches, extent, cells), jnp.bfloat16),
            pltpu.VMEM((cells // packed(extent), LANES), jnp.float32),
            pltpu.VMEM((cells // packed(extent), LANES), jnp.float32),
            pltpu.VMEM((extent, cells), jnp.float32),
            pltpu.VMEM((extent, extent // packed(extent) * LANES), jnp.float32),
            pltpu.VMEM((extent, cells), jnp.float32),
            pltpu.VMEM((extent, cells), jnp.float32),
            pltpu.SemaphoreType.DMA((1 + len(operands),)),
            pltpu.SemaphoreType.DMA((matches, pieces)),
            pltpu.SemaphoreType.DMA((matches, pieces)),
        ],
        compiler_params=pltpu.CompilerParams(
            collective_id=0, has_side_effects=True, vmem_limit_bytes=40 * 1024 * 1024
        ),
        name="exchange",
    )(*(pltpu.with_memory_space_constraint(one, pltpu.HBM) for one in (orbitals.reshape(extent, cells), *operands)))
    return exchange.reshape(1, extent, cells)


def solution(mesh):
    placed = (P("orb", None, None), P(), P())
    return jax.shard_map(
        per_device, mesh=mesh, in_specs=placed, out_specs=P("orb", None, None), check_vma=False
    )
```

```python
import functools
import math

import jax
import jax.numpy as jnp
import ml_dtypes
import numpy as np
from jax import lax
from jax.experimental import pallas as pl
from jax.experimental.pallas import tpu as pltpu
from jax.sharding import PartitionSpec as P

screening = 0.5
MESH = pl.DeviceIdType.MESH
LANES = 128


def split(values):
    high = values.astype(jnp.bfloat16)
    low = (values - high.astype(jnp.float32)).astype(jnp.bfloat16)
    return high, low


def split_constant(values):
    high = values.astype(ml_dtypes.bfloat16)
    low = (values - high.astype(np.float64)).astype(ml_dtypes.bfloat16)
    return high, low


def packed(extent):
    pack = LANES // extent
    while extent % (8 * pack):
        pack -= 1
    return pack


def tables(extent):
    modes = np.arange(1, extent + 1, dtype=np.float64)
    sines = math.sqrt(2.0 / (extent + 1)) * np.sin(
        math.pi * modes[:, None] * modes[None, :] / (extent + 1)
    )
    eigenvalue = 2.0 - 2.0 * np.cos(math.pi * modes / (extent + 1))
    pack = packed(extent)
    padded = np.zeros((LANES, LANES))
    padded[: pack * extent, : pack * extent] = np.kron(np.eye(pack), sines)
    tiles = extent // pack
    last = np.zeros((tiles, LANES))
    for at in range(pack):
        first = eigenvalue[at * tiles : (at + 1) * tiles]
        last[:, at * extent : (at + 1) * extent] = first[:, None] + eigenvalue[None, :]
    eigen_lane = (last + screening).reshape(1, tiles * LANES)
    eigen_row = np.broadcast_to(eigenvalue[:, None], (extent, LANES))
    lane = np.arange(extent * extent)
    places = np.stack([lane // extent, lane % extent]).astype(np.int32)
    return (
        *split_constant(sines),
        *split_constant(padded),
        eigen_row.astype(np.float32),
        eigen_lane.astype(np.float32),
        places,
    )


def kernel(
    strides,
    pieces,
    orbital_ref,
    *refs,
):
    count = (len(refs) - 12) // 2
    sources, out_ref, held = refs[:count], refs[count], refs[count + 1 : 2 * count + 1]
    own, arrived, rows_in, rows_out, flat, symbol, moved_own, moved_theirs, load_sem, send_sem, recv_sem = refs[
        2 * count + 1 :
    ]
    offsets_ref, mask_ref, sines_high_ref, sines_low_ref, padded_high_ref, padded_low_ref = held[:6]
    eigen_row_ref, eigen_lane_ref, places_ref = held[6:]
    extent, cells = own.shape
    width = math.lcm(extent, LANES)
    pieces = cells // width
    pack = packed(extent)
    tiles = extent // pack
    myself = lax.axis_index("orb")
    lows = [lax.rem(myself // stride, 2) == 0 for stride in strides]
    partners = [
        jnp.where(low, myself + stride, myself - stride) for low, stride in zip(lows, strides)
    ]

    loads = [
        pltpu.make_async_copy(source, target, load_sem.at[at])
        for at, (source, target) in enumerate(zip((orbital_ref, *sources), (own, *held)))
    ]
    barrier = pltpu.get_barrier_semaphore()
    for partner in partners:
        pl.semaphore_signal(barrier, inc=1, device_id={"orb": partner}, device_id_type=MESH)
    for load in loads:
        load.start()
    pl.semaphore_wait(barrier, len(strides))
    copies = [
        [
            pltpu.make_async_remote_copy(
                src_ref=orbital_ref.at[:, pl.ds(piece * width, width)],
                dst_ref=arrived.at[match_index, :, pl.ds(piece * width, width)],
                send_sem=send_sem.at[match_index, piece],
                recv_sem=recv_sem.at[match_index, piece],
                device_id={"orb": partners[match_index]},
                device_id_type=MESH,
            )
            for piece in range(pieces)
        ]
        for match_index in range(len(strides))
    ]
    far = len(strides) - 1
    early = pieces // 3
    yields = lax.rem(myself // max(strides[far] // 2, 1), 4) == 3

    def send(match_index, part=slice(None)):
        for copy in copies[match_index][part]:
            copy.start()

    @pl.when(jnp.logical_not(yields))
    def _():
        send(far)

    for match_index in range(far):
        send(match_index)
    for load in loads:
        load.wait()

    symbol[...] = 1.0 / (eigen_row_ref[:, :1] + eigen_lane_ref[...])
    per_width = width // extent

    def product(left, right):
        return jnp.dot(left, right, preferred_element_type=jnp.float32)

    def side_by_side(high, low):
        return jnp.concatenate([high, low, high], axis=1).astype(jnp.bfloat16)

    row = lax.broadcasted_iota(jnp.int32, (extent, extent), 0)
    column = lax.broadcasted_iota(jnp.int32, (extent, extent), 1)
    tile_row = lax.broadcasted_iota(jnp.int32, (LANES, LANES), 0)
    tile_column = lax.broadcasted_iota(jnp.int32, (LANES, LANES), 1)
    tile_minor = places_ref[1:2, :LANES]
    tile_block = places_ref[0:1, :LANES]

    def forward_table(amount):
        pick = jnp.where(row - column == amount, 1.0, 0.0).astype(jnp.bfloat16)
        return side_by_side(product(sines_high_ref[...], pick), product(sines_low_ref[...], pick))

    def inverse_table(amount):
        pick = jnp.where(column - row == amount, 1.0, 0.0).astype(jnp.bfloat16)
        return side_by_side(product(pick, sines_high_ref[...]), product(pick, sines_low_ref[...]))

    def lane_table(high, low):
        high, low = high.astype(jnp.bfloat16), low.astype(jnp.bfloat16)
        upper = jnp.concatenate([high, low], axis=1)
        return jnp.concatenate([upper, jnp.concatenate([high, jnp.zeros_like(low)], axis=1)], axis=0)

    def forward_lanes(amount):
        inside = (tile_minor >= amount) & (tile_minor < extent + amount)
        pick = (tile_column - tile_row == amount) & inside
        pick = jnp.where(pick, 1.0, 0.0).astype(jnp.bfloat16)
        return lane_table(product(pick, padded_high_ref[...]), product(pick, padded_low_ref[...]))

    def inverse_lanes(amount):
        inside = (tile_minor >= -amount) & (tile_minor < extent - amount)
        pick = (tile_row - tile_column == amount) & inside
        pick = jnp.where(pick, 1.0, 0.0).astype(jnp.bfloat16)
        return lane_table(product(padded_high_ref[...], pick), product(padded_low_ref[...], pick))

    def contract_rows(table, volume, rounded=False):
        if rounded:
            high = volume.astype(jnp.bfloat16)
            return product(table[:, : 2 * extent], jnp.concatenate([high, high], axis=0))
        high, low = split(volume)
        return product(table, jnp.concatenate([high, high, low], axis=0))

    def contract_lanes(table, volume, rounded=False):
        if rounded:
            both = product(volume.astype(jnp.bfloat16), table[:LANES])
        else:
            both = product(jnp.concatenate(split(volume), axis=1), table)
        return both[:, :LANES] + both[:, LANES:]

    def shift_rows(volume, amount):
        pick = jnp.where(row - column == amount, 1.0, 0.0).astype(jnp.bfloat16)
        return product(pick, volume)

    def shift_lanes(moved, offset):
        turn = offset[1] * extent + offset[2]
        moved = pltpu.roll(moved, jnp.where(turn < 0, turn + cells, turn), 1)
        middle = places_ref[0:1, :] - offset[1]
        minor = places_ref[1:2, :] - offset[2]
        inside = (middle >= 0) & (middle < extent) & (minor >= 0) & (minor < extent)
        return jnp.where(inside, moved, 0.0)

    total = None
    for match_index, stride in enumerate(strides):
        is_low = lows[match_index]
        lower = jnp.where(is_low, myself, myself - stride)
        live = mask_ref[match_index, lower]
        offset = [offsets_ref[axis, match_index, lower] for axis in range(3)]
        ahead = [jnp.where(is_low, value, 0) for value in offset]
        behind = [jnp.where(is_low, 0, value) for value in offset]
        outward = [jnp.where(is_low, -value, value) for value in offset]
        inward = [-value for value in outward]
        moved_own[...] = shift_lanes(shift_rows(own[...], outward[0]), outward)
        rows_forward, middle_forward = forward_table(ahead[0]), forward_table(ahead[1])
        rows_inverse, middle_inverse = inverse_table(behind[0]), inverse_table(behind[1])
        lanes_forward, lanes_inverse = forward_lanes(ahead[2]), inverse_lanes(behind[2])

        if match_index == min(1, far):

            @pl.when(yields)
            def _():
                send(far, slice(early if far else 0, None))

        for piece, copy in enumerate(copies[match_index]):
            copy.wait_recv()
            span = slice(piece * width, (piece + 1) * width)
            theirs = arrived[match_index, :, span]
            moved_theirs[:, span] = shift_rows(theirs, inward[0])
            density = theirs.astype(jnp.float32) * moved_own[:, span]
            part = contract_rows(rows_forward, density)
            part = jnp.concatenate([part[:, -LANES:], part, part[:, :LANES]], axis=1)
            slabs = []
            for at in range(per_width):
                slab = None
                for lap in range(pack):
                    start = LANES + (at - lap) * extent
                    window = part[lap * tiles : (lap + 1) * tiles, start : start + LANES]
                    slab = window if slab is None else jnp.where(tile_block < lap, slab, window)
                slabs.append(slab)
            part = contract_lanes(lanes_forward, jnp.concatenate(slabs, axis=0))
            for at in range(per_width):
                rows_in[pl.ds(piece * per_width + at, tiles, stride=extent), :] = part[
                    at * tiles : (at + 1) * tiles
                ]
        if match_index < min(1, far):

            @pl.when(yields)
            def _():
                send(far, slice(early))

        volume = jnp.concatenate(
            [rows_in[at * extent : (at + 1) * extent, :] for at in range(tiles)], axis=1
        )
        volume = symbol[...] * contract_rows(middle_forward, volume)
        volume = contract_rows(middle_inverse, volume, rounded=True)
        volume = jnp.concatenate(
            [volume[:, at * LANES : (at + 1) * LANES] for at in range(tiles)], axis=0
        )
        rows_out[...] = contract_lanes(lanes_inverse, volume, rounded=True)
        for at in range(extent):
            slab = rows_out[pl.ds(at, tiles, stride=extent), :]
            for lap in range(pack):
                flat[lap * tiles : (lap + 1) * tiles, at * extent : (at + 1) * extent] = slab[
                    :, lap * extent : (lap + 1) * extent
                ]
        potential = contract_rows(rows_inverse, flat[...])
        visitor = shift_lanes(moved_theirs[...], inward)
        term = (potential * visitor).astype(jnp.bfloat16).astype(jnp.float32)
        term = jnp.where(live > 0, term, 0.0)
        total = term if total is None else total + term
    out_ref[...] = (-total).astype(out_ref.dtype)
    for started in copies:
        for copy in started:
            copy.wait_send()


def per_device(orbitals, pair_mask, offsets):
    extent, cells = orbitals.shape[1:]
    levels = lax.axis_size("orb").bit_length() - 1
    matches = pair_mask.shape[0]
    strides = [1 << match_index * (levels - 1) // (matches - 1) for match_index in range(matches)]
    pieces = cells // math.lcm(extent, LANES)
    operands = (offsets, pair_mask, *map(jnp.asarray, tables(extent)))
    spaces = [pltpu.SMEM] * 2 + [pltpu.VMEM] * (len(operands) - 2)
    exchange = pl.pallas_call(
        functools.partial(kernel, strides, pieces),
        out_shape=pltpu.VMEM((extent, cells), jnp.bfloat16),
        in_specs=[pl.BlockSpec(memory_space=pltpu.HBM)] * (1 + len(operands)),
        out_specs=pl.BlockSpec(memory_space=pltpu.VMEM),
        scratch_shapes=[space(one.shape, one.dtype) for space, one in zip(spaces, operands)]
        + [
            pltpu.VMEM((extent, cells), jnp.bfloat16),
            pltpu.VMEM((matches, extent, cells), jnp.bfloat16),
            pltpu.VMEM((cells // packed(extent), LANES), jnp.float32),
            pltpu.VMEM((cells // packed(extent), LANES), jnp.float32),
            pltpu.VMEM((extent, cells), jnp.float32),
            pltpu.VMEM((extent, extent // packed(extent) * LANES), jnp.float32),
            pltpu.VMEM((extent, cells), jnp.float32),
            pltpu.VMEM((extent, cells), jnp.float32),
            pltpu.SemaphoreType.DMA((1 + len(operands),)),
            pltpu.SemaphoreType.DMA((matches, pieces)),
            pltpu.SemaphoreType.DMA((matches, pieces)),
        ],
        compiler_params=pltpu.CompilerParams(
            collective_id=0, has_side_effects=True, vmem_limit_bytes=40 * 1024 * 1024
        ),
        name="exchange",
    )(*(pltpu.with_memory_space_constraint(one, pltpu.HBM) for one in (orbitals.reshape(extent, cells), *operands)))
    return exchange.reshape(1, extent, cells)


def solution(mesh):
    placed = (P("orb", None, None), P(), P())
    return jax.shard_map(
        per_device, mesh=mesh, in_specs=placed, out_specs=P("orb", None, None), check_vma=False
    )
```

```python
import functools
import math

import jax
import jax.numpy as jnp
import ml_dtypes
import numpy as np
from jax import lax
from jax.experimental import pallas as pl
from jax.experimental.pallas import tpu as pltpu
from jax.sharding import PartitionSpec as P

screening = 0.5
MESH = pl.DeviceIdType.MESH
LANES = 128


def split(values):
    high = values.astype(jnp.bfloat16)
    low = (values - high.astype(jnp.float32)).astype(jnp.bfloat16)
    return high, low


def split_constant(values):
    high = values.astype(ml_dtypes.bfloat16)
    low = (values - high.astype(np.float64)).astype(ml_dtypes.bfloat16)
    return high, low


def packed(extent):
    pack = LANES // extent
    while extent % (8 * pack):
        pack -= 1
    return pack


def tables(extent):
    modes = np.arange(1, extent + 1, dtype=np.float64)
    sines = math.sqrt(2.0 / (extent + 1)) * np.sin(
        math.pi * modes[:, None] * modes[None, :] / (extent + 1)
    )
    eigenvalue = 2.0 - 2.0 * np.cos(math.pi * modes / (extent + 1))
    pack = packed(extent)
    padded = np.zeros((LANES, LANES))
    padded[: pack * extent, : pack * extent] = np.kron(np.eye(pack), sines)
    tiles = extent // pack
    last = np.zeros((tiles, LANES))
    for at in range(pack):
        first = eigenvalue[at * tiles : (at + 1) * tiles]
        last[:, at * extent : (at + 1) * extent] = first[:, None] + eigenvalue[None, :]
    eigen_lane = (last + screening).reshape(1, tiles * LANES)
    eigen_row = np.broadcast_to(eigenvalue[:, None], (extent, LANES))
    lane = np.arange(extent * extent)
    places = np.stack([lane // extent, lane % extent]).astype(np.int32)
    return (
        *split_constant(sines),
        *split_constant(padded),
        eigen_row.astype(np.float32),
        eigen_lane.astype(np.float32),
        places,
    )


def kernel(
    strides,
    pieces,
    orbital_ref,
    *refs,
):
    count = (len(refs) - 12) // 2
    sources, out_ref, held = refs[:count], refs[count], refs[count + 1 : 2 * count + 1]
    own, arrived, rows_in, rows_out, flat, symbol, moved_own, moved_theirs, load_sem, send_sem, recv_sem = refs[
        2 * count + 1 :
    ]
    offsets_ref, mask_ref, sines_high_ref, sines_low_ref, padded_high_ref, padded_low_ref = held[:6]
    eigen_row_ref, eigen_lane_ref, places_ref = held[6:]
    extent, cells = own.shape
    width = math.lcm(extent, LANES)
    pieces = cells // width
    pack = packed(extent)
    tiles = extent // pack
    myself = lax.axis_index("orb")
    lows = [lax.rem(myself // stride, 2) == 0 for stride in strides]
    partners = [
        jnp.where(low, myself + stride, myself - stride) for low, stride in zip(lows, strides)
    ]

    loads = [
        pltpu.make_async_copy(source, target, load_sem.at[at])
        for at, (source, target) in enumerate(zip((orbital_ref, *sources), (own, *held)))
    ]
    barrier = pltpu.get_barrier_semaphore()
    for partner in partners:
        pl.semaphore_signal(barrier, inc=1, device_id={"orb": partner}, device_id_type=MESH)
    for load in loads:
        load.start()
    pl.semaphore_wait(barrier, len(strides))
    copies = [
        [
            pltpu.make_async_remote_copy(
                src_ref=orbital_ref.at[:, pl.ds(piece * width, width)],
                dst_ref=arrived.at[match_index, :, pl.ds(piece * width, width)],
                send_sem=send_sem.at[match_index, piece],
                recv_sem=recv_sem.at[match_index, piece],
                device_id={"orb": partners[match_index]},
                device_id_type=MESH,
            )
            for piece in range(pieces)
        ]
        for match_index in range(len(strides))
    ]
    far = len(strides) - 1
    early = pieces // 3
    yields = lax.rem(myself // max(strides[far] // 2, 1), 4) == 3

    def send(match_index, part=slice(None)):
        for copy in copies[match_index][part]:
            copy.start()

    @pl.when(jnp.logical_not(yields))
    def _():
        send(far)

    for match_index in range(far):
        send(match_index)
    for load in loads:
        load.wait()

    symbol[...] = 1.0 / (eigen_row_ref[:, :1] + eigen_lane_ref[...])
    per_width = width // extent

    def product(left, right):
        return jnp.dot(left, right, preferred_element_type=jnp.float32)

    def side_by_side(high, low):
        return jnp.concatenate([high, low, high], axis=1).astype(jnp.bfloat16)

    row = lax.broadcasted_iota(jnp.int32, (extent, extent), 0)
    column = lax.broadcasted_iota(jnp.int32, (extent, extent), 1)
    tile_row = lax.broadcasted_iota(jnp.int32, (LANES, LANES), 0)
    tile_column = lax.broadcasted_iota(jnp.int32, (LANES, LANES), 1)
    tile_minor = places_ref[1:2, :LANES]
    tile_block = places_ref[0:1, :LANES]

    def forward_table(amount):
        pick = jnp.where(row - column == amount, 1.0, 0.0).astype(jnp.bfloat16)
        return side_by_side(product(sines_high_ref[...], pick), product(sines_low_ref[...], pick))

    def inverse_table(amount):
        pick = jnp.where(column - row == amount, 1.0, 0.0).astype(jnp.bfloat16)
        return side_by_side(product(pick, sines_high_ref[...]), product(pick, sines_low_ref[...]))

    def lane_table(high, low):
        high, low = high.astype(jnp.bfloat16), low.astype(jnp.bfloat16)
        upper = jnp.concatenate([high, low], axis=1)
        return jnp.concatenate([upper, jnp.concatenate([high, jnp.zeros_like(low)], axis=1)], axis=0)

    def forward_lanes(amount):
        inside = (tile_minor >= amount) & (tile_minor < extent + amount)
        pick = (tile_column - tile_row == amount) & inside
        pick = jnp.where(pick, 1.0, 0.0).astype(jnp.bfloat16)
        return lane_table(product(pick, padded_high_ref[...]), product(pick, padded_low_ref[...]))

    def inverse_lanes(amount):
        inside = (tile_minor >= -amount) & (tile_minor < extent - amount)
        pick = (tile_row - tile_column == amount) & inside
        pick = jnp.where(pick, 1.0, 0.0).astype(jnp.bfloat16)
        return lane_table(product(padded_high_ref[...], pick), product(padded_low_ref[...], pick))

    def contract_rows(table, volume):
        high, low = split(volume)
        return product(table, jnp.concatenate([high, high, low], axis=0))

    def contract_lanes(table, volume):
        both = product(jnp.concatenate(split(volume), axis=1), table)
        return both[:, :LANES] + both[:, LANES:]

    def shift_rows(volume, amount):
        pick = jnp.where(row - column == amount, 1.0, 0.0).astype(jnp.bfloat16)
        return product(pick, volume)

    def shift_lanes(moved, offset):
        turn = offset[1] * extent + offset[2]
        moved = pltpu.roll(moved, jnp.where(turn < 0, turn + cells, turn), 1)
        middle = places_ref[0:1, :] - offset[1]
        minor = places_ref[1:2, :] - offset[2]
        inside = (middle >= 0) & (middle < extent) & (minor >= 0) & (minor < extent)
        return jnp.where(inside, moved, 0.0)

    total = None
    for match_index, stride in enumerate(strides):
        is_low = lows[match_index]
        lower = jnp.where(is_low, myself, myself - stride)
        live = mask_ref[match_index, lower]
        offset = [offsets_ref[axis, match_index, lower] for axis in range(3)]
        ahead = [jnp.where(is_low, value, 0) for value in offset]
        behind = [jnp.where(is_low, 0, value) for value in offset]
        outward = [jnp.where(is_low, -value, value) for value in offset]
        inward = [-value for value in outward]
        moved_own[...] = shift_lanes(shift_rows(own[...], outward[0]), outward)
        rows_forward, middle_forward = forward_table(ahead[0]), forward_table(ahead[1])
        rows_inverse, middle_inverse = inverse_table(behind[0]), inverse_table(behind[1])
        lanes_forward, lanes_inverse = forward_lanes(ahead[2]), inverse_lanes(behind[2])

        if match_index == min(1, far):

            @pl.when(yields)
            def _():
                send(far, slice(early if far else 0, None))

        for piece, copy in enumerate(copies[match_index]):
            copy.wait_recv()
            span = slice(piece * width, (piece + 1) * width)
            theirs = arrived[match_index, :, span]
            moved_theirs[:, span] = shift_rows(theirs, inward[0])
            density = theirs.astype(jnp.float32) * moved_own[:, span]
            part = contract_rows(rows_forward, density)
            part = jnp.concatenate([part[:, -LANES:], part, part[:, :LANES]], axis=1)
            slabs = []
            for at in range(per_width):
                slab = None
                for lap in range(pack):
                    start = LANES + (at - lap) * extent
                    window = part[lap * tiles : (lap + 1) * tiles, start : start + LANES]
                    slab = window if slab is None else jnp.where(tile_block < lap, slab, window)
                slabs.append(slab)
            part = contract_lanes(lanes_forward, jnp.concatenate(slabs, axis=0))
            for at in range(per_width):
                rows_in[pl.ds(piece * per_width + at, tiles, stride=extent), :] = part[
                    at * tiles : (at + 1) * tiles
                ]
        if match_index < min(1, far):

            @pl.when(yields)
            def _():
                send(far, slice(early))

        volume = jnp.concatenate(
            [rows_in[at * extent : (at + 1) * extent, :] for at in range(tiles)], axis=1
        )
        volume = symbol[...] * contract_rows(middle_forward, volume)
        volume = contract_rows(middle_inverse, volume)
        volume = jnp.concatenate(
            [volume[:, at * LANES : (at + 1) * LANES] for at in range(tiles)], axis=0
        )
        rows_out[...] = contract_lanes(lanes_inverse, volume)
        for at in range(extent):
            slab = rows_out[pl.ds(at, tiles, stride=extent), :]
            for lap in range(pack):
                flat[lap * tiles : (lap + 1) * tiles, at * extent : (at + 1) * extent] = slab[
                    :, lap * extent : (lap + 1) * extent
                ]
        potential = jnp.concatenate(
            [
                contract_rows(rows_inverse, flat[:, at * width : (at + 1) * width])
                for at in range(pieces)
            ],
            axis=1,
        )
        visitor = shift_lanes(moved_theirs[...], inward)
        term = (potential * visitor).astype(jnp.bfloat16).astype(jnp.float32)
        term = jnp.where(live > 0, term, 0.0)
        total = term if total is None else total + term
    out_ref[...] = (-total).astype(out_ref.dtype)
    for started in copies:
        for copy in started:
            copy.wait_send()


def per_device(orbitals, pair_mask, offsets):
    extent, cells = orbitals.shape[1:]
    levels = lax.axis_size("orb").bit_length() - 1
    matches = pair_mask.shape[0]
    strides = [1 << match_index * (levels - 1) // (matches - 1) for match_index in range(matches)]
    pieces = cells // math.lcm(extent, LANES)
    operands = (offsets, pair_mask, *map(jnp.asarray, tables(extent)))
    spaces = [pltpu.SMEM] * 2 + [pltpu.VMEM] * (len(operands) - 2)
    exchange = pl.pallas_call(
        functools.partial(kernel, strides, pieces),
        out_shape=pltpu.VMEM((extent, cells), jnp.bfloat16),
        in_specs=[pl.BlockSpec(memory_space=pltpu.HBM)] * (1 + len(operands)),
        out_specs=pl.BlockSpec(memory_space=pltpu.VMEM),
        scratch_shapes=[space(one.shape, one.dtype) for space, one in zip(spaces, operands)]
        + [
            pltpu.VMEM((extent, cells), jnp.bfloat16),
            pltpu.VMEM((matches, extent, cells), jnp.bfloat16),
            pltpu.VMEM((cells // packed(extent), LANES), jnp.float32),
            pltpu.VMEM((cells // packed(extent), LANES), jnp.float32),
            pltpu.VMEM((extent, cells), jnp.float32),
            pltpu.VMEM((extent, extent // packed(extent) * LANES), jnp.float32),
            pltpu.VMEM((extent, cells), jnp.float32),
            pltpu.VMEM((extent, cells), jnp.float32),
            pltpu.SemaphoreType.DMA((1 + len(operands),)),
            pltpu.SemaphoreType.DMA((matches, pieces)),
            pltpu.SemaphoreType.DMA((matches, pieces)),
        ],
        compiler_params=pltpu.CompilerParams(
            collective_id=0, has_side_effects=True, vmem_limit_bytes=40 * 1024 * 1024
        ),
        name="exchange",
    )(*(pltpu.with_memory_space_constraint(one, pltpu.HBM) for one in (orbitals.reshape(extent, cells), *operands)))
    return exchange.reshape(1, extent, cells)


def solution(mesh):
    placed = (P("orb", None, None), P(), P())
    return jax.shard_map(
        per_device, mesh=mesh, in_specs=placed, out_specs=P("orb", None, None), check_vma=False
    )
```
